256 devices in a mesh: gx: 32 (over x_hi, z, core), gy: 8 (over x_lo, y).
Axes of the slice: x: 4 (x_hi: 2, x_lo: 2; x = x_hi * 2 + x_lo), y: 4, z: 8, core: 2. Of those that a mesh axis runs over, the one named last changes fastest.
Arguments:
- tokens: bfloat16 [448, 112, 14, 192], P('gx', 'gy'), may hold values from -6 to 6
- qkv_weight: bfloat16 [192, 576], replicated, may hold values from -1.299038 to 1.299038
- proj_weight: bfloat16 [192, 192], replicated, may hold values from -0.4375 to 0.4375
- merge_weight: bfloat16 [1536, 384], replicated, may hold values from -0.15625 to 0.15625
- cotangent: bfloat16 [224, 56, 7, 384], P('gx', 'gy'), may hold values from -6 to 6
Outputs:
- token_grad: bfloat16 [448, 112, 14, 192], P('gx', 'gy')
- qkv_grad: float32 [192, 576], replicated
- proj_grad: float32 [192, 192], replicated
- merge_grad: float32 [1536, 384], replicated
The draws below stay inside these ranges and needn't reach their ends.
All inputs are finite; a program needn't handle non-finite values.
Results may differ from the reference program's by a relative error of at most 0.03.
The reference program's roundings to bfloat16 on the way count: a program that leaves them out, or rounds other values in their place, can miss the bound.
Values may be sent and summed in bfloat16 or wider, within the bound.
No kernel may reach another device: no remote copies, remote signals or barrier semaphores. Data moves between devices by JAX's collectives and lax.ppermute only.
A program may use at most 128 MiB of HBM per device.

```python
import jax
import jax.numpy as jnp
from jax import lax

C = 192
HEADS = 12
HD = 16
WIN = 7
SHIFT = 3
NW = 14
ND = 448
NH = 112


def draw_qkv_weight(key, part):
    key = jax.random.fold_in(key, 7)
    first = jax.random.fold_in(key, 0)
    unit = C ** (-0.5)
    base = jax.random.truncated_normal(first, -4.0, 4.0, (C, 3 * C), jnp.float32) * unit
    return jnp.clip(base, -18.0 * unit, 18.0 * unit).astype(jnp.bfloat16)


def block_scale(key, extent, pieces, low, top_value):
    loudness, own = 1.0, jax.random.fold_in(key, 6)
    for position, shards_of in pieces:
        draws = jnp.exp(jax.random.uniform(jax.random.fold_in(own, position), (shards_of,), jnp.float32, low / len(pieces), top_value / len(pieces)))
        loudness = loudness * jnp.repeat(draws, extent[position] // shards_of).reshape([-1 if axis == position else 1 for axis in range(len(extent))])
    return loudness


def centred(stream_key, extent, scale, bound, shards=(), held_as=jnp.bfloat16):
    loudness = block_scale(stream_key, extent, shards, -0.22, 0.18) if shards else 1.0
    result = jax.random.normal(stream_key, extent, jnp.float32) * scale * loudness
    return jnp.minimum(jnp.maximum(result, -bound), bound).astype(held_as)


def setup_inputs(seed: int = 0) -> dict:
    key_of = jax.random.split(jax.random.key(seed), 6)
    return {
        "tokens": centred(key_of[0], (ND, NH, NW, C), 1.0, 6.0, ((0, 32), (1, 8))),
        "qkv_weight": draw_qkv_weight(jax.random.fold_in(key_of[5], 71), 0),
        "proj_weight": centred(key_of[2], (C, C), C ** -0.5, 0.4375),
        "merge_weight": centred(key_of[3], (8 * C, 2 * C), (8 * C) ** -0.5, 0.15625),
        "cotangent": centred(key_of[4], (ND // 2, NH // 2, NW // 2, 2 * C), 1.0, 6.0, ((0, 32), (1, 8))),
    }


EPSILON = 1e-05

def norm_rows(values):
    centre = values - lax.optimization_barrier(jnp.mean(values, axis=-1, keepdims=True))
    inv_std = lax.rsqrt(lax.optimization_barrier(jnp.mean(centre * centre, axis=-1, keepdims=True)) + EPSILON)
    return (centre * inv_std, inv_std)

def norm_back(grad, normed, inv_std):
    return inv_std * (grad - lax.optimization_barrier(jnp.mean(grad, axis=-1, keepdims=True)) - normed * lax.optimization_barrier(jnp.mean(grad * normed, axis=-1, keepdims=True)))

def region_of(positions, total):
    return jnp.where(positions < total - WIN, 0, jnp.where(positions < total - SHIFT, 1, 2)).astype(jnp.int32)

def to_windows(grid):
    depth, height, width, feats = grid.shape
    grid = grid.reshape(depth // WIN, WIN, height // WIN, WIN, width // WIN, WIN, feats)
    return grid.transpose(0, 2, 4, 1, 3, 5, 6).reshape(-1, WIN ** 3, feats)

def from_windows(blocks, depth, height, width):
    feats = blocks.shape[-1]
    grid = blocks.reshape(depth // WIN, height // WIN, width // WIN, WIN, WIN, WIN, feats)
    return grid.transpose(0, 3, 1, 4, 2, 5, 6).reshape(depth, height, width, feats)

def merge_groups(grid):
    depth, height, width, feats = grid.shape
    grid = grid.reshape(depth // 2, 2, height // 2, 2, width // 2, 2, feats)
    return grid.transpose(0, 2, 4, 1, 3, 5, 6).reshape(depth // 2, height // 2, width // 2, 8 * feats)

def split_groups(grid, feats):
    half_d, half_h, half_w, wide = grid.shape
    grid = grid.reshape(half_d, half_h, half_w, 2, 2, 2, feats)
    return grid.transpose(0, 3, 1, 4, 2, 5, 6).reshape(2 * half_d, 2 * half_h, 2 * half_w, feats)

def rounded(values):
    return lax.optimization_barrier(values.astype(jnp.bfloat16)).astype(jnp.float32)

def attention_probs(query, keys, marks):
    scores = jnp.einsum('qhd,khd->hqk', query, keys) * HD ** (-0.5)
    same = marks[:, None] == marks[None, :]
    scores = jnp.where(same[None], scores, -1e+30)
    top = lax.optimization_barrier(jnp.max(scores, axis=-1, keepdims=True))
    expo = jnp.exp(scores - top)
    return expo / lax.optimization_barrier(jnp.sum(expo, axis=-1, keepdims=True))

def reference(tokens, qkv_weight, proj_weight, merge_weight, cotangent):
    depth, height, width, feats = tokens.shape
    tokens_f = tokens.astype(jnp.float32)
    normed, inv_std = norm_rows(tokens_f)
    shifted = jnp.roll(normed.astype(jnp.bfloat16), (-SHIFT, -SHIFT, -SHIFT), axis=(0, 1, 2))
    labels = (region_of(jnp.arange(depth), depth)[:, None, None] * 9 + region_of(jnp.arange(height), height)[None, :, None] * 3 + region_of(jnp.arange(width), width)[None, None, :]).astype(jnp.int32)
    win_in = to_windows(shifted)
    win_lab = to_windows(labels[..., None])[..., 0]

    def window_qkv(block):
        qkv = jnp.dot(block, qkv_weight, preferred_element_type=jnp.float32)
        return rounded(qkv).reshape(-1, 3, HEADS, HD)

    def forward_window(item):
        block, marks = item
        qkv = window_qkv(block)
        probs = attention_probs(qkv[:, 0], qkv[:, 1], marks)
        mixed = jnp.einsum('hqk,khd->qhd', rounded(probs), qkv[:, 2])
        return mixed.reshape(-1, feats).astype(jnp.bfloat16)
    attn_out = from_windows(lax.map(forward_window, (win_in, win_lab)), depth, height, width)
    attn_rows = attn_out.reshape(-1, feats)
    projected = jnp.dot(attn_rows, proj_weight, preferred_element_type=jnp.float32).astype(jnp.bfloat16)
    projected = jnp.roll(projected.reshape(depth, height, width, feats), (SHIFT, SHIFT, SHIFT), axis=(0, 1, 2))
    block_out = (tokens_f + projected.astype(jnp.float32)).astype(jnp.bfloat16)
    merged = merge_groups(block_out).astype(jnp.float32).reshape(-1, 8 * feats)
    merged_norm, inv_std_m = norm_rows(merged)
    cot_rows = cotangent.reshape(-1, 2 * feats)
    merge_grad = jnp.dot(merged_norm.astype(jnp.bfloat16).T, cot_rows, preferred_element_type=jnp.float32)
    grad_mnorm = jnp.dot(cot_rows, merge_weight.T, preferred_element_type=jnp.float32)
    grad_merged = norm_back(grad_mnorm, merged_norm, inv_std_m)
    grad_block = split_groups(grad_merged.reshape(depth // 2, height // 2, width // 2, 8 * feats), feats)
    grad_rolled = jnp.roll(grad_block.astype(jnp.bfloat16), (-SHIFT, -SHIFT, -SHIFT), axis=(0, 1, 2))
    grad_rows = grad_rolled.reshape(-1, feats)
    proj_grad = jnp.dot(attn_rows.T, grad_rows, preferred_element_type=jnp.float32)
    grad_attn = jnp.dot(grad_rows, proj_weight.T, preferred_element_type=jnp.float32).astype(jnp.bfloat16)
    win_grad = to_windows(grad_attn.reshape(depth, height, width, feats))

    def backward_window(item):
        block, marks, grad_out = item
        qkv = window_qkv(block)
        query, keys, values = (qkv[:, 0], qkv[:, 1], qkv[:, 2])
        probs = attention_probs(query, keys, marks)
        grad_o = grad_out.astype(jnp.float32).reshape(-1, HEADS, HD)
        grad_probs = jnp.einsum('qhd,khd->hqk', grad_o, values)
        grad_values = jnp.einsum('hqk,qhd->khd', rounded(probs), grad_o)
        grad_scores = probs * (grad_probs - lax.optimization_barrier(jnp.sum(probs * grad_probs, axis=-1, keepdims=True)))
        grad_scores = rounded(grad_scores)
        grad_query = jnp.einsum('hqk,khd->qhd', grad_scores, keys) * HD ** (-0.5)
        grad_keys = jnp.einsum('hqk,qhd->khd', grad_scores, query) * HD ** (-0.5)
        stacked = jnp.stack([grad_query, grad_keys, grad_values], axis=1)
        return stacked.reshape(-1, 3 * feats).astype(jnp.bfloat16)
    grad_qkv = from_windows(lax.map(backward_window, (win_in, win_lab, win_grad)), depth, height, width)
    grad_qkv_rows = grad_qkv.reshape(-1, 3 * feats)
    qkv_grad = jnp.dot(shifted.reshape(-1, feats).T, grad_qkv_rows, preferred_element_type=jnp.float32)
    grad_shifted = jnp.dot(grad_qkv_rows, qkv_weight.T, preferred_element_type=jnp.float32).astype(jnp.bfloat16)
    grad_normed = jnp.roll(grad_shifted.reshape(depth, height, width, feats), (SHIFT, SHIFT, SHIFT), axis=(0, 1, 2))
    token_grad = grad_block + norm_back(grad_normed.astype(jnp.float32), normed, inv_std)
    return (token_grad.astype(jnp.bfloat16), qkv_grad, proj_grad, merge_grad)
```

```python
import jax
import jax.numpy as jnp
import numpy as np
from jax import lax
from jax.experimental import pallas as pl
from jax.experimental.pallas import tpu as pltpu
from jax.sharding import PartitionSpec as P

C = 192
HEADS = 12
HD = 16
WIN = 7
SHIFT = 3
SIDE = 14
WPAD = 16
TOK = WIN**3
ROWS = 352
LROWS = 384
WIDE = 256
GROUP = WIN * WIN * WPAD
STAT = 192
LABEL = 228
CLASSES = 8
FAR = 1e30
EPSILON = 1e-05
BF = jnp.bfloat16
F32 = jnp.float32
VMEM_LIMIT = 60 * 2**20


def head_masks():
    mask = np.zeros((HEADS, WIDE), np.float32)
    for head in range(HEADS):
        mask[head, head * HD : (head + 1) * HD] = 1
        for part in range(3):
            mask[head, STAT + part * HEADS + head] = 1
        mask[head, LABEL : LABEL + CLASSES] = 1
    return mask


def head_spread():
    spread = np.zeros((WIDE, WIDE), np.float32)
    for head in range(HEADS):
        for part in range(3):
            spread[head * HD : (head + 1) * HD, STAT + part * HEADS + head] = 1
    return spread


def head_expand():
    expand = np.zeros((WIDE, WIDE), np.float32)
    for head in range(HEADS):
        expand[STAT + head, head * HD : (head + 1) * HD] = 1
    return expand


def window_gather():
    gather = np.zeros((2 * ROWS, GROUP), np.float32)
    for half in range(2):
        for pair in range(WIN * WIN):
            for place in range(WIN):
                width = (half * WIN + place + SHIFT) % SIDE
                gather[half * ROWS + pair * WIN + place, pair * WPAD + width] = 1
    return gather


def parity_gather():
    gather = np.zeros((2 * ROWS, GROUP), np.float32)
    for parity in range(2):
        for pair in range(WIN * WIN):
            for place in range(WIN):
                gather[parity * ROWS + pair * WIN + place, pair * WPAD + 2 * place + parity] = 1
    return gather


def class_codes():
    codes = np.full((LROWS, 1), CLASSES, np.int32)
    for place in range(TOK):
        i, j, k = place // (WIN * WIN), place // WIN % WIN, place % WIN
        codes[place, 0] = 4 * (i >= 4) + 2 * (j >= 4) + (k >= 4)
    return codes


def dot(a, b):
    return lax.dot_general(a, b, (((1,), (0,)), ((), ())), preferred_element_type=F32)


def dot_nt(a, b):
    return lax.dot_general(a, b, (((1,), (1,)), ((), ())), preferred_element_type=F32)


def dot_tn(a, b):
    return lax.dot_general(a, b, (((0,), (0,)), ((), ())), preferred_element_type=F32)


def three_parts(value):
    high = value.astype(BF)
    rest = value - high.astype(F32)
    middle = rest.astype(BF)
    low = (rest - middle.astype(F32)).astype(BF)
    return high, middle, low


def dot_exact(value, table):
    high, middle, low = three_parts(value)
    return dot(high, table) + dot(middle, table) + dot(low, table)


def stat_lanes(value, lane):
    high, middle, low = three_parts(value)
    mixed = jnp.where(
        lane < STAT + HEADS,
        high.astype(F32),
        jnp.where(lane < STAT + 2 * HEADS, middle.astype(F32), low.astype(F32)),
    )
    return jnp.where((lane >= STAT) & (lane < STAT + 3 * HEADS), mixed, 0.0)


def norm_rows(values):
    centre = values - jnp.mean(values, axis=-1, keepdims=True)
    inv_std = lax.rsqrt(jnp.mean(centre * centre, axis=-1, keepdims=True) + EPSILON)
    return (centre * inv_std, inv_std)


def place_rolled(rolled, own, ahead_d, ahead_h, ahead_dh):
    keep = SIDE - SHIFT
    rolled[:, :, SIDE:, :] = jnp.zeros((SIDE, SIDE, WPAD - SIDE, C), rolled.dtype)
    rolled[0:keep, 0:keep, 0:SIDE, :] = own[SHIFT:, SHIFT:, :, :]
    rolled[keep:, 0:keep, 0:SIDE, :] = ahead_d[...]
    rolled[0:keep, keep:, 0:SIDE, :] = ahead_h[...]
    rolled[keep:, keep:, 0:SIDE, :] = ahead_dh[...]


def window_rows(rolled, first_d, first_h):
    block = rolled[pl.ds(first_d * WIN, WIN), pl.ds(first_h * WIN, WIN), :, :]
    return block.reshape(GROUP, C)


def forward_kernel(
    edges,
    own,
    ahead_d,
    ahead_h,
    ahead_dh,
    wqkv,
    wproj,
    gather,
    scatter,
    codes,
    masks,
    expand,
    out,
    rows_out,
    q_out,
    k_out,
    v_out,
    mixed_out,
    rolled,
):
    wd, wh = pl.program_id(0), pl.program_id(1)

    @pl.when((wd == 0) & (wh == 0))
    def _():
        place_rolled(rolled, own, ahead_d, ahead_h, ahead_dh)

    lane = lax.broadcasted_iota(jnp.int32, (1, WIDE), 1)
    normed, _ = norm_rows(window_rows(rolled, wd, wh).astype(F32))
    both = dot(gather[...], normed.astype(BF)).astype(BF)
    mixed_halves = []
    for half in range(2):
        rows = both[half * ROWS : (half + 1) * ROWS]
        rows_out[half] = rows
        q = dot(rows, wqkv[0])
        k = dot(rows, wqkv[1])
        v = dot(rows, wqkv[2])
        allowed = (
            4 * jnp.where(wd == 1, edges[0], 0)
            + 2 * jnp.where(wh == 1, edges[1], 0)
            + half
            + CLASSES
        )
        own_class = LABEL + (codes[...] & allowed)
        here = lane == own_class
        in_labels = (lane >= LABEL) & (lane < LABEL + CLASSES)
        in_stats = (lane >= STAT) & (lane < STAT + 3 * HEADS)
        zeros = jnp.zeros((LROWS - ROWS, WIDE), F32)
        q = jnp.concatenate([q, zeros], axis=0)
        k = jnp.concatenate([k, zeros], axis=0)
        q_aug = jnp.where(in_labels, jnp.where(here, 1.0, 0.0), q).astype(BF)
        k_aug = jnp.where(
            in_labels, jnp.where(here, 0.0, -FAR), jnp.where(in_stats, -1.0, k)
        ).astype(BF)
        v_aug = jnp.where(in_stats, -1.0, v).astype(BF)
        v_wide = jnp.concatenate([v_aug, jnp.zeros((LROWS - ROWS, WIDE), BF)], axis=0)
        total = jnp.zeros((ROWS, WIDE), F32)
        tops = jnp.zeros((ROWS, WIDE), F32)
        for head in range(HEADS):
            mask = masks[head : head + 1, :]
            scores = dot_nt(q_aug[:ROWS], k_aug * mask)
            top = jnp.max(scores, axis=-1, keepdims=True)
            expo = jnp.exp(scores - top).astype(BF)
            total = total + dot(expo, v_wide * mask)
            tops = jnp.where(masks[head : head + 1, :].astype(F32) > 0, top, tops)
        sums = jnp.where(in_stats, -total, 1.0)
        mixed = total * dot_exact(jnp.where(in_stats, 1.0 / sums, 0.0), expand[...])
        mixed_out[half] = mixed
        stats = jnp.where(in_stats, tops + jnp.log(sums), 0.0)
        q_out[half, 0:ROWS] = (q_aug[:ROWS].astype(F32) + stat_lanes(stats, lane)).astype(BF)
        q_out[half, ROWS:] = q_aug[ROWS:]
        k_out[half] = k_aug
        v_out[half] = v_aug
        mixed_halves.append(dot(mixed[:, :C].astype(BF), wproj[...]).astype(BF))
    back = dot(scatter[...], jnp.concatenate(mixed_halves, axis=0)).astype(BF)
    out[...] = back.reshape(WIN, WIN, WPAD, C)[:, :, :SIDE, :]


def backward_kernel(
    own,
    ahead_d,
    ahead_h,
    ahead_dh,
    rows_in,
    q_in,
    k_in,
    v_in,
    mixed_in,
    wqkv,
    wproj,
    gather,
    scatter,
    masks,
    spread,
    out,
    qkv_part,
    proj_part,
    rolled,
    dqt,
):
    wd, wh = pl.program_id(0), pl.program_id(1)

    @pl.when((wd == 0) & (wh == 0))
    def _():
        place_rolled(rolled, own, ahead_d, ahead_h, ahead_dh)
        qkv_part[...] = jnp.zeros_like(qkv_part)
        proj_part[...] = jnp.zeros_like(proj_part)

    lane = lax.broadcasted_iota(jnp.int32, (1, WIDE), 1)
    both = dot(gather[...], window_rows(rolled, wd, wh)).astype(BF)
    back_halves = []
    for half in range(2):
        grads = both[half * ROWS : (half + 1) * ROWS]
        mixed = mixed_in[half]
        proj_part[...] += dot_tn(mixed[:, :C].astype(BF), grads)
        grad_o = dot_nt(grads, wproj[...]).astype(BF)
        delta = dot_exact(mixed * grad_o.astype(F32), spread[...])
        o_aug = (grad_o.astype(F32) + stat_lanes(delta, lane)).astype(BF)
        o_aug = jnp.concatenate([o_aug, jnp.zeros((LROWS - ROWS, WIDE), BF)], axis=0)
        q_aug = q_in[half]
        k_aug = k_in[half][:ROWS]
        v_aug = v_in[half]
        k_t = k_aug[:, :C].astype(F32).T.astype(BF)
        grad_k = jnp.zeros((ROWS, WIDE), F32)
        grad_v = jnp.zeros((ROWS, WIDE), F32)
        for head in range(HEADS):
            mask = masks[head : head + 1, :]
            q_m = q_aug * mask
            o_m = o_aug * mask
            probs = jnp.exp(dot_nt(k_aug, q_m))
            slopes = (probs * dot_nt(v_aug, o_m)).astype(BF)
            grad_v = grad_v + dot(probs.astype(BF), o_m)
            grad_k = grad_k + dot(slopes, q_m)
            dqt[head * HD : (head + 1) * HD, :] = dot(
                k_t[head * HD : (head + 1) * HD, :], slopes
            )
        grad_q = (dqt[...].T[:ROWS] * HD**-0.5).astype(BF)
        grad_k = grad_k[:, :C].astype(BF)
        grad_v = grad_v[:, :C].astype(BF)
        rows = rows_in[half]
        shifted = jnp.zeros((ROWS, C), F32)
        for part, grad in enumerate((grad_q, grad_k, grad_v)):
            qkv_part[part] += dot_tn(rows, grad)
            shifted = shifted + dot_nt(grad, wqkv[part])
        back_halves.append(shifted.astype(BF))
    back = dot(scatter[...], jnp.concatenate(back_halves, axis=0)).astype(BF)
    out[...] = back.reshape(WIN, WIN, WPAD, C)[:, :, :SIDE, :]


def whole(shape):
    return pl.BlockSpec(shape, lambda wd, wh: (0,) * len(shape))


def per_step(shape):
    return pl.BlockSpec(shape, lambda wd, wh: (2 * wd + wh,) + (0,) * (len(shape) - 1))


def grid_block():
    return pl.BlockSpec((WIN, WIN, SIDE, C), lambda wd, wh: (wd, wh, 0, 0))


KEEP = SIDE - SHIFT
SLABS = ((SHIFT, KEEP, SIDE, C), (KEEP, SHIFT, SIDE, C), (SHIFT, SHIFT, SIDE, C))
PARAMS = pltpu.CompilerParams(
    dimension_semantics=("arbitrary", "arbitrary"), vmem_limit_bytes=VMEM_LIMIT
)


def forward_call(edges, grid, slabs, wqkv, wproj, consts):
    struct = jax.ShapeDtypeStruct
    return pl.pallas_call(
        forward_kernel,
        grid=(2, 2),
        in_specs=[
            pl.BlockSpec(memory_space=pltpu.SMEM),
            whole((SIDE, SIDE, SIDE, C)),
            *[whole(s) for s in SLABS],
            whole((3, C, WIDE)),
            whole((C, C)),
            whole((2 * ROWS, GROUP)),
            whole((GROUP, 2 * ROWS)),
            whole((LROWS, 1)),
            whole((HEADS, WIDE)),
            whole((WIDE, WIDE)),
        ],
        out_specs=[
            grid_block(),
            per_step((2, ROWS, C)),
            per_step((2, LROWS, WIDE)),
            per_step((2, LROWS, WIDE)),
            per_step((2, ROWS, WIDE)),
            per_step((2, ROWS, WIDE)),
        ],
        out_shape=[
            struct((SIDE, SIDE, SIDE, C), BF),
            struct((8, ROWS, C), BF),
            struct((8, LROWS, WIDE), BF),
            struct((8, LROWS, WIDE), BF),
            struct((8, ROWS, WIDE), BF),
            struct((8, ROWS, WIDE), F32),
        ],
        scratch_shapes=[pltpu.VMEM((SIDE, SIDE, WPAD, C), BF)],
        compiler_params=PARAMS,
        name="window_forward",
    )(
        edges,
        grid,
        *slabs,
        wqkv,
        wproj,
        consts["gather"],
        consts["scatter"],
        consts["codes"],
        consts["masks"],
        consts["expand"],
    )


def backward_call(grid, slabs, saved, wqkv, wproj_wide, consts):
    struct = jax.ShapeDtypeStruct
    return pl.pallas_call(
        backward_kernel,
        grid=(2, 2),
        in_specs=[
            whole((SIDE, SIDE, SIDE, C)),
            *[whole(s) for s in SLABS],
            per_step((2, ROWS, C)),
            per_step((2, LROWS, WIDE)),
            per_step((2, LROWS, WIDE)),
            per_step((2, ROWS, WIDE)),
            per_step((2, ROWS, WIDE)),
            whole((3, C, C)),
            whole((WIDE, C)),
            whole((2 * ROWS, GROUP)),
            whole((GROUP, 2 * ROWS)),
            whole((HEADS, WIDE)),
            whole((WIDE, WIDE)),
        ],
        out_specs=[grid_block(), whole((3, C, C)), whole((C, C))],
        out_shape=[
            struct((SIDE, SIDE, SIDE, C), BF),
            struct((3, C, C), F32),
            struct((C, C), F32),
        ],
        scratch_shapes=[
            pltpu.VMEM((SIDE, SIDE, WPAD, C), BF),
            pltpu.VMEM((C, LROWS), F32),
        ],
        compiler_params=PARAMS,
        name="window_backward",
    )(
        grid,
        *slabs,
        *saved,
        wqkv,
        wproj_wide,
        consts["gather"],
        consts["scatter"],
        consts["masks"],
        consts["spread"],
    )


def place_trailing(target, own, behind_d, behind_h, behind_dh):
    target[SHIFT:, SHIFT:, 0:SIDE, :] = own[0:KEEP, 0:KEEP, :, :]
    target[0:SHIFT, SHIFT:, 0:SIDE, :] = behind_d[...]
    target[SHIFT:, 0:SHIFT, 0:SIDE, :] = behind_h[...]
    target[0:SHIFT, 0:SHIFT, 0:SIDE, :] = behind_dh[...]


def merge_kernel(
    tokens,
    own,
    behind_d,
    behind_h,
    behind_dh,
    cotangent,
    weight,
    gather,
    scatter,
    high_out,
    low_out,
    part_out,
    block,
    pieces,
):
    block[:, :, SIDE:, :] = jnp.zeros((SIDE, SIDE, WPAD - SIDE, C), BF)
    place_trailing(block, own, behind_d, behind_h, behind_dh)
    block[:, :, 0:SIDE, :] = (
        tokens[...].astype(F32) + block[:, :, 0:SIDE, :].astype(F32)
    ).astype(BF)
    total = jnp.zeros((ROWS, 1), F32)
    for pair in range(4):
        a, b = pair // 2, pair % 2
        part = block[...].reshape(WIN, 2, WIN, 2, WPAD, C)[:, a, :, b]
        both = dot(gather[...], part.reshape(GROUP, C))
        for c in range(2):
            piece = both[c * ROWS : (c + 1) * ROWS]
            pieces[2 * pair + c] = piece
            total = total + jnp.sum(piece, axis=-1, keepdims=True)
    mean = total / (8 * C)
    square = jnp.zeros((ROWS, 1), F32)
    for index in range(8):
        centre = pieces[index] - mean
        square = square + jnp.sum(centre * centre, axis=-1, keepdims=True)
    inv_std = lax.rsqrt(square / (8 * C) + EPSILON)
    grad_sum = jnp.zeros((ROWS, 1), F32)
    cross_sum = jnp.zeros((ROWS, 1), F32)
    cot = cotangent[...]
    for index in range(8):
        normed = (pieces[index] - mean) * inv_std
        part_out[index] = dot_tn(normed.astype(BF), cot)
        grad = dot_nt(cot, weight[index])
        grad_sum = grad_sum + jnp.sum(grad, axis=-1, keepdims=True)
        cross_sum = cross_sum + jnp.sum(grad * normed, axis=-1, keepdims=True)
    grad_mean = grad_sum / (8 * C)
    cross_mean = cross_sum / (8 * C)
    for a in range(2):
        highs, lows = [], []
        for b in range(2):
            high_pair, low_pair = [], []
            for c in range(2):
                index = 4 * a + 2 * b + c
                normed = (pieces[index] - mean) * inv_std
                grad = dot_nt(cot, weight[index])
                grad = inv_std * (grad - grad_mean - normed * cross_mean)
                high = grad.astype(BF)
                high_pair.append(high)
                low_pair.append((grad - high.astype(F32)).astype(BF))
            for pair, kept in ((high_pair, highs), (low_pair, lows)):
                laid = dot(scatter[...], jnp.concatenate(pair, axis=0)).astype(BF)
                kept.append(laid.reshape(WIN, WIN, WPAD, C))
        for kept, out in ((highs, high_out), (lows, low_out)):
            merged = jnp.stack(kept, axis=2).reshape(WIN, SIDE, WPAD, C)
            for i in range(WIN):
                out[2 * i + a] = merged[i, :, :SIDE, :]


def final_kernel(tokens, high, low, own, behind_d, behind_h, behind_dh, out, grads):
    place_trailing(grads, own, behind_d, behind_h, behind_dh)

    @pl.loop(0, SIDE)
    def _(d):
        normed, inv_std = norm_rows(tokens[d].astype(F32))
        grad = grads[d].astype(F32)
        back = inv_std * (
            grad
            - jnp.mean(grad, axis=-1, keepdims=True)
            - normed * jnp.mean(grad * normed, axis=-1, keepdims=True)
        )
        out[d] = (high[d].astype(F32) + low[d].astype(F32) + back).astype(BF)


def merge_call(tokens, own, slabs, cot_rows, weight, consts):
    struct = jax.ShapeDtypeStruct
    grid = (SIDE, SIDE, SIDE, C)
    return pl.pallas_call(
        merge_kernel,
        out_shape=[
            struct(grid, BF),
            struct(grid, BF),
            struct((8, C, 2 * C), F32),
        ],
        scratch_shapes=[
            pltpu.VMEM((SIDE, SIDE, WPAD, C), BF),
            pltpu.VMEM((8, ROWS, C), F32),
        ],
        compiler_params=pltpu.CompilerParams(vmem_limit_bytes=VMEM_LIMIT),
        name="merge_backward",
    )(tokens, own, *slabs, cot_rows, weight, consts["pair_gather"], consts["pair_scatter"])


def final_call(tokens, high, low, own, slabs):
    grid = (SIDE, SIDE, SIDE, C)
    return pl.pallas_call(
        final_kernel,
        out_shape=jax.ShapeDtypeStruct(grid, BF),
        scratch_shapes=[pltpu.VMEM(grid, BF)],
        compiler_params=pltpu.CompilerParams(vmem_limit_bytes=VMEM_LIMIT),
        name="token_gradient",
    )(tokens, high, low, own, *slabs)


def moved(value, steps_d, steps_h):
    count_d, count_h = lax.axis_size("gx"), lax.axis_size("gy")
    pairs = []
    for d in range(count_d):
        for h in range(count_h):
            target = (d + steps_d) % count_d * count_h + (h + steps_h) % count_h
            pairs.append((d * count_h + h, target))
    return lax.ppermute(value, ("gx", "gy"), pairs)


def slabs_ahead(grid):
    return (
        moved(grid[:SHIFT, SHIFT:], -1, 0),
        moved(grid[SHIFT:, :SHIFT], 0, -1),
        moved(grid[:SHIFT, :SHIFT], -1, -1),
    )


def slabs_behind(grid):
    return (
        moved(grid[KEEP:, :KEEP], 1, 0),
        moved(grid[:KEEP, KEEP:], 0, 1),
        moved(grid[KEEP:, KEEP:], 1, 1),
    )


def summed(part):
    axes = ("gx", "gy")
    count = lax.axis_size(axes)
    shape = part.shape
    blocks = part.astype(BF).reshape(count, part.size // count)
    blocks = lax.all_to_all(blocks, axes, 0, 0, tiled=True)
    own = jnp.sum(blocks.astype(F32), axis=0).astype(BF)
    spread = jnp.broadcast_to(own[None], blocks.shape)
    spread = lax.all_to_all(spread, axes, 0, 0, tiled=True)
    return spread.astype(F32).reshape(shape)


def wide(weight):
    return jnp.pad(weight, ((0, 0), (0, WIDE - weight.shape[1])))


def local(tokens, qkv_weight, proj_weight, merge_weight, cotangent):
    gather = window_gather()
    pair = parity_gather()
    consts = {
        "gather": jnp.asarray(gather, BF),
        "scatter": jnp.asarray(gather.T, BF),
        "pair_gather": jnp.asarray(pair, BF),
        "pair_scatter": jnp.asarray(pair.T, BF),
        "codes": jnp.asarray(class_codes()),
        "masks": jnp.asarray(head_masks(), BF),
        "expand": jnp.asarray(head_expand(), BF),
        "spread": jnp.asarray(head_spread(), BF),
    }
    edges = jnp.stack(
        [
            (lax.axis_index("gx") == lax.axis_size("gx") - 1).astype(jnp.int32),
            (lax.axis_index("gy") == lax.axis_size("gy") - 1).astype(jnp.int32),
        ]
    )
    wqkv = qkv_weight.reshape(C, 3, C).transpose(1, 0, 2)
    scaled = jnp.concatenate([wqkv[:1] * BF(HD**-0.5), wqkv[1:]], axis=0)
    scaled = jnp.pad(scaled, ((0, 0), (0, 0), (0, WIDE - C)))
    wproj_wide = jnp.pad(proj_weight, ((0, WIDE - C), (0, 0)))
    cot_rows = jnp.pad(cotangent.reshape(TOK, 2 * C), ((0, ROWS - TOK), (0, 0)))
    weight = merge_weight.reshape(8, C, 2 * C)

    projected, *saved = forward_call(
        edges, tokens, slabs_ahead(tokens), scaled, proj_weight, consts
    )
    high, low, merge_part = merge_call(
        tokens, projected, slabs_behind(projected), cot_rows, weight, consts
    )
    merge_grad = summed(merge_part.reshape(8 * C, 2 * C))
    grad_shifted, qkv_part, proj_part = backward_call(
        high, slabs_ahead(high), saved, wqkv, wproj_wide, consts
    )
    token_grad = final_call(tokens, high, low, grad_shifted, slabs_behind(grad_shifted))
    late = summed(jnp.concatenate([qkv_part, proj_part[None]], axis=0))
    qkv_grad = late[:3].transpose(1, 0, 2).reshape(C, 3 * C)
    return token_grad, qkv_grad, late[3], merge_grad


def solution(mesh):
    placed = (P("gx", "gy", None, None), P(), P(), P(), P("gx", "gy", None, None))
    return jax.shard_map(
        local,
        mesh=mesh,
        in_specs=placed,
        out_specs=(P("gx", "gy", None, None), P(), P(), P()),
        check_vma=False,
    )
```

```python
import jax
import jax.numpy as jnp
import numpy as np
from jax import lax
from jax.experimental import pallas as pl
from jax.experimental.pallas import tpu as pltpu
from jax.sharding import PartitionSpec as P

C = 192
HEADS = 12
HD = 16
WIN = 7
SHIFT = 3
SIDE = 14
WPAD = 16
TOK = WIN**3
ROWS = 352
LROWS = 384
WIDE = 256
GROUP = WIN * WIN * WPAD
TILE = 128
CHUNK = 16
SPAN = CHUNK * WIN
FULL = WIN * WIN // CHUNK
TILES = 6
MAIN = 4096
REST = 512
LATE = 2048
STAT = 192
LABEL = 228
CLASSES = 8
FAR = 1e30
EPSILON = 1e-05
BF = jnp.bfloat16
F32 = jnp.float32
VMEM_LIMIT = 40 * 2**20


def head_masks():
    mask = np.zeros((HEADS, WIDE), np.float32)
    for head in range(HEADS):
        mask[head, head * HD : (head + 1) * HD] = 1
        for part in range(3):
            mask[head, STAT + part * HEADS + head] = 1
        mask[head, LABEL : LABEL + CLASSES] = 1
    return mask


def head_spread():
    spread = np.zeros((WIDE, WIDE), np.float32)
    for head in range(HEADS):
        for part in range(3):
            spread[head * HD : (head + 1) * HD, STAT + part * HEADS + head] = 1
    return spread


def group_table(width_of):
    table = np.zeros((2, CHUNK * WIN, CHUNK * WPAD), np.float32)
    for half in range(2):
        for pair in range(CHUNK):
            for place in range(WIN):
                table[half, pair * WIN + place, pair * WPAD + width_of(half, place)] = 1
    return table.reshape(2 * CHUNK * WIN, CHUNK * WPAD)


def window_table():
    return group_table(lambda half, place: (half * WIN + place + SHIFT) % SIDE)


def parity_table():
    return group_table(lambda parity, place: 2 * place + parity)


def class_codes():
    codes = np.full((LROWS, 1), CLASSES, np.int32)
    for place in range(TOK):
        i, j, k = place // (WIN * WIN), place // WIN % WIN, place % WIN
        codes[place, 0] = 4 * (i >= 4) + 2 * (j >= 4) + (k >= 4)
    return codes


def dot(a, b):
    return lax.dot_general(a, b, (((1,), (0,)), ((), ())), preferred_element_type=F32)


def dot_nt(a, b):
    return lax.dot_general(a, b, (((1,), (1,)), ((), ())), preferred_element_type=F32)


def dot_tn(a, b):
    return lax.dot_general(a, b, (((0,), (0,)), ((), ())), preferred_element_type=F32)


def gather_groups(table, block):
    halves = ([], [])
    for chunk in range(FULL):
        start = chunk * CHUNK * WPAD
        both = dot(table[...], block[start : start + CHUNK * WPAD])
        for half in range(2):
            halves[half].append(both[half * SPAN : (half + 1) * SPAN])
    tail = jnp.concatenate([table[:WPAD, :TILE], table[SPAN : SPAN + WPAD, :TILE]], axis=0)
    end = block[FULL * CHUNK * WPAD :]
    end = jnp.concatenate([end, jnp.zeros((TILE - WPAD, end.shape[1]), end.dtype)], axis=0)
    both = dot(tail, end)
    for half in range(2):
        halves[half].append(both[half * WPAD : (half + 1) * WPAD])
    return [jnp.concatenate(rows, axis=0) for rows in halves]


def scatter_groups(table, halves):
    out = []
    for chunk in range(FULL):
        rows = slice(chunk * SPAN, (chunk + 1) * SPAN)
        out.append(dot(table[...], jnp.concatenate([h[rows] for h in halves], axis=0)))
    pad = jnp.zeros((SPAN - WPAD, halves[0].shape[1]), halves[0].dtype)
    tail = [part for h in halves for part in (h[FULL * SPAN :], pad)]
    out.append(dot(table[:WPAD, :], jnp.concatenate(tail, axis=0)))
    return jnp.concatenate(out, axis=0)


def three_parts(value):
    high = value.astype(BF)
    rest = value - high.astype(F32)
    middle = rest.astype(BF)
    low = (rest - middle.astype(F32)).astype(BF)
    return high, middle, low


def dot_exact(value, table):
    high, middle, low = three_parts(value)
    return dot(high, table) + dot(middle, table) + dot(low, table)


def stat_lanes(value, lane):
    high, middle, low = three_parts(value)
    mixed = jnp.where(
        lane < STAT + HEADS,
        high.astype(F32),
        jnp.where(lane < STAT + 2 * HEADS, middle.astype(F32), low.astype(F32)),
    )
    return jnp.where((lane >= STAT) & (lane < STAT + 3 * HEADS), mixed, 0.0)


def norm_rows(values):
    centre = values - jnp.mean(values, axis=-1, keepdims=True)
    inv_std = lax.rsqrt(jnp.mean(centre * centre, axis=-1, keepdims=True) + EPSILON)
    return (centre * inv_std, inv_std)


def place_rolled(rolled, own, ahead_d, ahead_h, ahead_dh):
    keep = SIDE - SHIFT
    rolled[:, :, SIDE:, :] = jnp.zeros((SIDE, SIDE, WPAD - SIDE, C), rolled.dtype)
    rolled[0:keep, 0:keep, 0:SIDE, :] = own[SHIFT:, SHIFT:, :, :]
    rolled[keep:, 0:keep, 0:SIDE, :] = ahead_d[...]
    rolled[0:keep, keep:, 0:SIDE, :] = ahead_h[...]
    rolled[keep:, keep:, 0:SIDE, :] = ahead_dh[...]


def pair_corner(pair):
    return WIN * lax.div(pair, 2), WIN * lax.rem(pair, 2)


def forward_pair(
    wd,
    wh,
    block,
    edges,
    wqkv,
    wturned,
    wproj,
    gather,
    scatter,
    codes,
    masks,
    rows_out,
    q_out,
    k_out,
    kt_out,
    v_out,
    mixed_out,
    mixed_t,
    stat_t,
):
    lane = lax.broadcasted_iota(jnp.int32, (1, WIDE), 1)
    in_labels = (lane >= LABEL) & (lane < LABEL + CLASSES)
    in_stats = (lane >= STAT) & (lane < STAT + 3 * HEADS)
    normed, _ = norm_rows(block.reshape(GROUP, C).astype(F32))
    pad = jnp.zeros((LROWS - ROWS, C), BF)
    both = gather_groups(gather, normed.astype(BF))
    halves = []
    for half in range(2):
        rows = jnp.concatenate([both[half].astype(BF), pad], axis=0)
        rows_out[half] = rows[:ROWS]
        q = dot(rows, wqkv[0])
        k = dot(rows, wqkv[1])
        v = dot(rows, wqkv[2])
        kt_out[half] = dot_nt(wturned[0], rows).astype(BF)[:, :ROWS]
        vt = dot_nt(wturned[1], rows).astype(BF)[:, :ROWS]
        allowed = (
            4 * jnp.where(wd == 1, edges[0], 0)
            + 2 * jnp.where(wh == 1, edges[1], 0)
            + half
            + CLASSES
        )
        here = lane == LABEL + (codes[...] & allowed)
        q_aug = jnp.where(in_labels, jnp.where(here, 1.0, 0.0), q).astype(BF)
        k_aug = jnp.where(
            in_labels, jnp.where(here, 0.0, -FAR), jnp.where(in_stats, -1.0, k)
        ).astype(BF)[:ROWS]
        v_aug = jnp.where(in_stats, -1.0, v).astype(BF)[:ROWS]
        stat_t[half] = jnp.zeros((WIDE - TILE, LROWS), F32)
        for two in range(HEADS // 2):
            q_m = jnp.concatenate(
                [q_aug * masks[h : h + 1, :] for h in (2 * two, 2 * two + 1)], axis=0
            )
            scores = dot_nt(k_aug, q_m)
            top = jnp.max(scores, axis=0, keepdims=True)
            expo = jnp.exp(scores - top)
            sums = jnp.sum(expo, axis=0, keepdims=True)
            probs = (expo * (1.0 / sums)).astype(BF)
            stats = top + jnp.log(sums)
            mixed = dot(vt[2 * HD * two : 2 * HD * (two + 1)], probs)
            for i in range(2):
                h = 2 * two + i
                lanes = slice(i * LROWS, (i + 1) * LROWS)
                mixed_t[half, h * HD : (h + 1) * HD, :] = mixed[i * HD : (i + 1) * HD, lanes]
                for part in range(3):
                    row = STAT - TILE + part * HEADS + h
                    stat_t[half, row : row + 1, :] = stats[:, lanes]
        mixed = mixed_t[half].T[:ROWS]
        mixed_out[half] = mixed
        q_out[half, :, :TILE] = q_aug[:, :TILE]
        stats = stat_lanes(stat_t[half].T, lane[:, TILE:])
        q_out[half, :, TILE:] = (q_aug[:, TILE:].astype(F32) + stats).astype(BF)
        k_out[half] = k_aug
        v_out[half] = v_aug
        halves.append(dot(mixed.astype(BF), wproj[...]).astype(BF))
    back = scatter_groups(scatter, halves).astype(BF)
    return back.reshape(WIN, WIN, WPAD, C)[:, :, :SIDE, :]


def first_block(block, own):
    block[:, :, SIDE:, :] = jnp.zeros((WIN, WIN, WPAD - SIDE, C), BF)
    block[:, :, 0:SIDE, :] = own[SHIFT : SHIFT + WIN, SHIFT : SHIFT + WIN, :, :]
    return block[...]


def forward_first(edges, own, *refs):
    *weights, out, rows, q, k, kt, v, mixed, block, mixed_t, stat_t = refs
    out[0] = forward_pair(
        0, 0, first_block(block, own), edges, *weights, rows, q, k, kt, v, mixed, mixed_t, stat_t
    )


def forward_rest(edges, own, ahead_d, ahead_h, ahead_dh, *refs):
    (
        *weights,
        out,
        slab_d,
        slab_h,
        slab_dh,
        rows,
        q,
        k,
        kt,
        v,
        mixed,
        rolled,
        mixed_t,
        stat_t,
    ) = refs
    pair = pl.program_id(0) + 1

    @pl.when(pair == 1)
    def _():
        place_rolled(rolled, own, ahead_d, ahead_h, ahead_dh)

    at_d, at_h = pair_corner(pair)
    block = rolled[pl.ds(at_d, WIN), pl.ds(at_h, WIN), :, :]
    out[0] = forward_pair(
        lax.div(pair, 2),
        lax.rem(pair, 2),
        block,
        edges,
        *weights,
        rows,
        q,
        k,
        kt,
        v,
        mixed,
        mixed_t,
        stat_t,
    )
    split = KEEP - WIN

    @pl.when(pair == 1)
    def _():
        slab_h[0:WIN] = out[0, :, split:]

    @pl.when(pair == 2)
    def _():
        slab_d[:, 0:WIN] = out[0, split:]

    @pl.when(pair == 3)
    def _():
        slab_h[WIN:] = out[0, :split, split:]
        slab_d[:, WIN:] = out[0, split:, :split]
        slab_dh[...] = out[0, split:, split:]


def backward_pair(
    block,
    rows_in,
    q_in,
    k_in,
    kt_in,
    v_in,
    mixed_in,
    wqkv,
    wproj,
    gather,
    scatter,
    masks,
    spread,
    qkv_sum,
    proj_sum,
    grad_t,
):
    lane = lax.broadcasted_iota(jnp.int32, (1, WIDE), 1)
    pad = jnp.zeros((LROWS - ROWS, C), BF)
    both = gather_groups(gather, block.reshape(GROUP, C))
    halves = []
    for half in range(2):
        grads = jnp.concatenate([both[half].astype(BF), pad], axis=0)
        mixed = mixed_in[half]
        proj_sum[...] += dot_tn(mixed.astype(BF), grads[:ROWS])
        grad_o = dot_nt(grads, wproj[...]).astype(BF)
        delta = dot_exact(mixed * grad_o[:ROWS, :C].astype(F32), spread[...])
        delta = jnp.concatenate(
            [stat_lanes(delta, lane), jnp.zeros((LROWS - ROWS, WIDE), F32)], axis=0
        )
        o_aug = (grad_o.astype(F32) + delta).astype(BF)
        q_aug = q_in[half]
        k_aug = k_in[half]
        v_aug = v_in[half]
        grad_k = jnp.zeros((ROWS, WIDE), F32)
        grad_v = jnp.zeros((ROWS, WIDE), F32)
        for two in range(HEADS // 2):
            heads = (2 * two, 2 * two + 1)
            q_m = jnp.concatenate([q_aug * masks[h : h + 1, :] for h in heads], axis=0)
            o_m = jnp.concatenate([o_aug * masks[h : h + 1, :] for h in heads], axis=0)
            probs = jnp.exp(dot_nt(k_aug, q_m))
            slopes = (probs * dot_nt(v_aug, o_m)).astype(BF)
            grad_v = grad_v + dot(probs.astype(BF), o_m)
            grad_k = grad_k + dot(slopes, q_m)
            turned = dot(kt_in[half, 2 * HD * two : 2 * HD * (two + 1), :], slopes)
            for i, h in enumerate(heads):
                grad_t[half, h * HD : (h + 1) * HD, :] = turned[
                    i * HD : (i + 1) * HD, i * LROWS : (i + 1) * LROWS
                ]
        grad_q = (grad_t[half].T[:ROWS] * HD**-0.5).astype(BF)
        grad = jnp.concatenate(
            [grad_q, grad_k[:, :C].astype(BF), grad_v[:, :C].astype(BF)], axis=1
        )
        qkv_sum[...] += dot_tn(rows_in[half], grad)
        halves.append(dot_nt(grad, wqkv[...]).astype(BF))
    back = scatter_groups(scatter, halves).astype(BF)
    return back.reshape(WIN, WIN, WPAD, C)[:, :, :SIDE, :]


def backward_first(own, *refs):
    *inputs, out, qkv_sum, proj_sum, block, grad_t = refs
    qkv_sum[...] = jnp.zeros_like(qkv_sum)
    proj_sum[...] = jnp.zeros_like(proj_sum)
    out[0] = backward_pair(first_block(block, own), *inputs, qkv_sum, proj_sum, grad_t)


def backward_middle(own, ahead_d, ahead_h, ahead_dh, *refs):
    *inputs, qkv_in, proj_in, _, out, qkv_sum, proj_sum, rolled, grad_t = refs
    pair = pl.program_id(0) + 1

    @pl.when(pair == 1)
    def _():
        place_rolled(rolled, own, ahead_d, ahead_h, ahead_dh)
        qkv_sum[...] = qkv_in[...]
        proj_sum[...] = proj_in[...]

    at_d, at_h = pair_corner(pair)
    block = rolled[pl.ds(at_d, WIN), pl.ds(at_h, WIN), :, :]
    out[0] = backward_pair(block, *inputs, qkv_sum, proj_sum, grad_t)


def backward_last(own, ahead_d, ahead_h, ahead_dh, *refs):
    *inputs, qkv_in, proj_in, rest, _, out, late, rolled, grad_t, qkv_sum, proj_sum = refs
    place_rolled(rolled, own, ahead_d, ahead_h, ahead_dh)
    qkv_sum[...] = qkv_in[...]
    proj_sum[...] = proj_in[...]
    out[0] = backward_pair(rolled[WIN:, WIN:, :, :], *inputs, qkv_sum, proj_sum, grad_t)
    table = jnp.concatenate([qkv_sum[...], proj_sum[...]], axis=1).astype(BF)
    for tile in range(TILES):
        late[tile * C : (tile + 1) * C, :] = table[:, tile * TILE : (tile + 1) * TILE]
    late[TILES * C : TILES * C + REST, :] = rest[...]
    late[TILES * C + REST :, :] = jnp.zeros((LATE - TILES * C - REST, TILE), BF)


def whole(shape):
    return pl.BlockSpec(shape, lambda step: (0,) * len(shape))


def per_pair(shape, first=0):
    return pl.BlockSpec(shape, lambda step: (step + first,) + (0,) * (len(shape) - 1))


KEEP = SIDE - SHIFT
GRID = (SIDE, SIDE, SIDE, C)
SLABS = ((SHIFT, KEEP, SIDE, C), (KEEP, SHIFT, SIDE, C), (SHIFT, SHIFT, SIDE, C))
SAVED = (
    ((ROWS, C), BF),
    ((LROWS, WIDE), BF),
    ((ROWS, WIDE), BF),
    ((C, ROWS), BF),
    ((ROWS, WIDE), BF),
    ((ROWS, C), F32),
)
PAIR = (1, WIN, WIN, SIDE, C)


def struct(shape, dtype):
    return jax.ShapeDtypeStruct(shape, dtype)


def call(kernel, name, count, operands, in_specs, outs, scratch, gigaflops):
    return pl.pallas_call(
        kernel,
        grid=(count,),
        in_specs=in_specs,
        out_specs=[spec for spec, _ in outs],
        out_shape=[shape for _, shape in outs],
        scratch_shapes=scratch,
        compiler_params=pltpu.CompilerParams(
            dimension_semantics=("arbitrary",), vmem_limit_bytes=VMEM_LIMIT
        ),
        cost_estimate=pl.CostEstimate(
            flops=int(gigaflops * 1e9), bytes_accessed=8 * 2**20, transcendentals=0
        ),
        name=name,
    )(*operands)


def in_hbm(array):
    return pltpu.with_memory_space_constraint(array, pltpu.HBM)


def whole_specs(arrays):
    return [whole(a.shape) for a in arrays]


def forward_call(edges, grid, slabs, weights, count):
    saved = [
        (per_pair((2,) + shape), pltpu.HBM((2 * count,) + shape, dtype))
        for shape, dtype in SAVED
    ]
    out = [(per_pair(PAIR), struct((count,) + PAIR[1:], BF))]
    scratch = [pltpu.VMEM((2, C, LROWS), F32), pltpu.VMEM((2, WIDE - TILE, LROWS), F32)]
    if slabs:
        out += [(whole(s), struct(s, BF)) for s in SLABS]
        scratch = [pltpu.VMEM((SIDE, SIDE, WPAD, C), BF)] + scratch
    else:
        scratch = [pltpu.VMEM((WIN, WIN, WPAD, C), BF)] + scratch
    operands = [grid, *slabs, *weights]
    return call(
        forward_rest if slabs else forward_first,
        "window_forward_rest" if slabs else "window_forward_first",
        count,
        [edges] + operands,
        [pl.BlockSpec(memory_space=pltpu.SMEM)] + whole_specs(operands),
        out + saved,
        scratch,
        5.0 * count,
    )


def backward_call(kernel, name, grid, slabs, saved, skip, tables, extra, count, outs, scratch, after=None):
    lead = [grid, *slabs]
    specs = whole_specs(lead)
    specs += [per_pair((2,) + shape, skip) for shape, _ in SAVED]
    specs += whole_specs([*tables, *extra])
    side = SIDE if slabs else WIN
    scratch = [
        pltpu.VMEM((side, side, WPAD, C), BF),
        pltpu.VMEM((2, C, LROWS), F32),
        *scratch,
    ]
    outs = [(per_pair(PAIR), struct((count,) + PAIR[1:], BF))] + [
        (whole(o.shape), o) for o in outs
    ]
    operands = [*lead, *[in_hbm(s) for s in saved], *tables, *extra]
    if after is not None:
        operands.append(after)
        specs.append(pl.BlockSpec(memory_space=pl.ANY))
    return call(kernel, name, count, operands, specs, outs, scratch, 12.0 * count)


def place_trailing(target, first, rest, behind_d, behind_h, behind_dh):
    split = KEEP - WIN
    target[SHIFT : SHIFT + WIN, SHIFT : SHIFT + WIN, 0:SIDE, :] = first[0]
    target[SHIFT : SHIFT + WIN, SHIFT + WIN :, 0:SIDE, :] = rest[0][:, :split]
    target[SHIFT + WIN :, SHIFT : SHIFT + WIN, 0:SIDE, :] = rest[1][:split]
    target[SHIFT + WIN :, SHIFT + WIN :, 0:SIDE, :] = rest[2][:split, :split]
    target[0:SHIFT, SHIFT:, 0:SIDE, :] = behind_d[...]
    target[SHIFT:, 0:SHIFT, 0:SIDE, :] = behind_h[...]
    target[0:SHIFT, 0:SHIFT, 0:SIDE, :] = behind_dh[...]


def merge_kernel(
    tokens,
    first,
    rest,
    behind_d,
    behind_h,
    behind_dh,
    cotangent,
    weight,
    gather,
    scatter,
    high_out,
    low_out,
    main_out,
    rest_out,
    slab_d,
    slab_h,
    slab_dh,
    block,
    pieces,
):
    block[:, :, SIDE:, :] = jnp.zeros((SIDE, SIDE, WPAD - SIDE, C), BF)
    place_trailing(block, first, rest, behind_d, behind_h, behind_dh)
    block[:, :, 0:SIDE, :] = (
        tokens[...].astype(F32) + block[:, :, 0:SIDE, :].astype(F32)
    ).astype(BF)
    total = jnp.zeros((ROWS, 1), F32)
    for pair in range(4):
        a, b = pair // 2, pair % 2
        part = block[...].reshape(WIN, 2, WIN, 2, WPAD, C)[:, a, :, b]
        both = gather_groups(gather, part.reshape(GROUP, C))
        for c in range(2):
            piece = both[c]
            pieces[2 * pair + c] = piece
            total = total + jnp.sum(piece, axis=-1, keepdims=True)
    mean = total / (8 * C)
    square = jnp.zeros((ROWS, 1), F32)
    for index in range(8):
        centre = pieces[index] - mean
        square = square + jnp.sum(centre * centre, axis=-1, keepdims=True)
    inv_std = lax.rsqrt(square / (8 * C) + EPSILON)
    grad_sum = jnp.zeros((ROWS, 1), F32)
    cross_sum = jnp.zeros((ROWS, 1), F32)
    cot = cotangent[...]
    for index in range(8):
        normed = (pieces[index] - mean) * inv_std
        part = dot_tn(normed.astype(BF), cot).astype(BF)
        for tile in range(3):
            start = tile * 8 * C + index * C
            keep = max(0, min(C, MAIN - start))
            columns = part[:, tile * TILE : (tile + 1) * TILE]
            if keep:
                main_out[start : start + keep, :] = columns[:keep]
            if keep < C:
                at = start + keep - MAIN
                rest_out[at : at + C - keep, :] = columns[keep:]
        grad = dot_nt(cot, weight[index])
        grad_sum = grad_sum + jnp.sum(grad, axis=-1, keepdims=True)
        cross_sum = cross_sum + jnp.sum(grad * normed, axis=-1, keepdims=True)
    grad_mean = grad_sum / (8 * C)
    cross_mean = cross_sum / (8 * C)
    for a in range(2):
        highs, lows = [], []
        for b in range(2):
            high_pair, low_pair = [], []
            for c in range(2):
                index = 4 * a + 2 * b + c
                normed = (pieces[index] - mean) * inv_std
                grad = dot_nt(cot, weight[index])
                grad = inv_std * (grad - grad_mean - normed * cross_mean)
                high = grad.astype(BF)
                high_pair.append(high)
                low_pair.append((grad - high.astype(F32)).astype(BF))
            for pair, kept in ((high_pair, highs), (low_pair, lows)):
                laid = scatter_groups(scatter, pair).astype(BF)
                kept.append(laid.reshape(WIN, WIN, WPAD, C))
        for kept, out in ((highs, high_out), (lows, low_out)):
            merged = jnp.stack(kept, axis=2).reshape(WIN, SIDE, WPAD, C)
            for i in range(WIN):
                out[2 * i + a] = merged[i, :, :SIDE, :]
    slab_d[...] = high_out[:SHIFT, SHIFT:]
    slab_h[...] = high_out[SHIFT:, :SHIFT]
    slab_dh[...] = high_out[:SHIFT, :SHIFT]


def final_kernel(
    tokens, high, low, first, middle, last, behind_d, behind_h, behind_dh, _, out, grads
):
    place_trailing(
        grads, first, (middle[0], middle[1], last[0]), behind_d, behind_h, behind_dh
    )

    @pl.loop(0, SIDE)
    def row(d):
        normed, inv_std = norm_rows(tokens[d].astype(F32))
        grad = grads[d].astype(F32)
        back = inv_std * (
            grad
            - jnp.mean(grad, axis=-1, keepdims=True)
            - normed * jnp.mean(grad * normed, axis=-1, keepdims=True)
        )
        out[d] = (high[d].astype(F32) + low[d].astype(F32) + back).astype(BF)


def merge_call(tokens, first, rest, slabs, cot_rows, weight, parity):
    operands = [in_hbm(tokens), first, rest, *slabs, cot_rows, in_hbm(weight), *parity]
    shapes = [GRID, GRID, (MAIN, TILE), (REST, TILE), *SLABS]
    kinds = [struct, pltpu.HBM, struct, pltpu.HBM, struct, struct, struct]
    return call(
        merge_kernel,
        "merge_backward",
        1,
        operands,
        whole_specs(operands),
        [(whole(s), kind(s, BF)) for s, kind in zip(shapes, kinds)],
        [pltpu.VMEM((SIDE, SIDE, WPAD, C), BF), pltpu.VMEM((8, ROWS, C), F32)],
        10.0,
    )


def final_call(tokens, high, low, first, middle, last, slabs, after):
    operands = [in_hbm(tokens), in_hbm(high), in_hbm(low), first, middle, last, *slabs]
    return call(
        final_kernel,
        "token_gradient",
        1,
        operands + [after],
        whole_specs(operands) + [pl.BlockSpec(memory_space=pl.ANY)],
        [(whole(GRID), struct(GRID, BF))],
        [pltpu.VMEM(GRID, BF)],
        7.0,
    )[0]


def moved(value, steps_d, steps_h):
    count_d, count_h = lax.axis_size("gx"), lax.axis_size("gy")
    pairs = []
    for d in range(count_d):
        for h in range(count_h):
            target = (d + steps_d) % count_d * count_h + (h + steps_h) % count_h
            pairs.append((d * count_h + h, target))
    return lax.ppermute(value, ("gx", "gy"), pairs)


def sent_back(slabs):
    d, h, dh = slabs
    return moved(d, -1, 0), moved(h, 0, -1), moved(dh, -1, -1)


def sent_on(slabs):
    d, h, dh = slabs
    return moved(d, 1, 0), moved(h, 0, 1), moved(dh, 1, 1)


def exchanged(blocks):
    return lax.all_to_all(blocks, ("gx", "gy"), 0, 0, tiled=True)


def block_sum(part):
    count = lax.axis_size(("gx", "gy"))
    blocks = exchanged(part.reshape(count, part.shape[0] // count, TILE))
    return jnp.sum(blocks.astype(F32), axis=0).astype(BF)


def block_spread(own):
    count = lax.axis_size(("gx", "gy"))
    spread = exchanged(jnp.broadcast_to(own[None], (count,) + own.shape))
    return spread.reshape(count * own.shape[0], TILE)


def local(tokens, qkv_weight, proj_weight, merge_weight, cotangent):
    gather = jnp.asarray(window_table(), BF)
    scatter = jnp.asarray(window_table().T, BF)
    parity = (jnp.asarray(parity_table(), BF), jnp.asarray(parity_table().T, BF))
    codes = jnp.asarray(class_codes())
    masks = jnp.asarray(head_masks(), BF)
    spread = jnp.asarray(head_spread()[:C], BF)
    edges = jnp.stack(
        [
            (lax.axis_index("gx") == lax.axis_size("gx") - 1).astype(jnp.int32),
            (lax.axis_index("gy") == lax.axis_size("gy") - 1).astype(jnp.int32),
        ]
    )
    split = qkv_weight.reshape(C, 3, C).transpose(1, 0, 2)
    scaled = jnp.concatenate([split[:1] * BF(HD**-0.5), split[1:]], axis=0)
    scaled = jnp.pad(scaled, ((0, 0), (0, 0), (0, WIDE - C)))
    turned = split[1:].transpose(0, 2, 1)
    wproj_wide = jnp.pad(proj_weight, ((0, WIDE - C), (0, 0)))
    cot_rows = jnp.pad(cotangent.reshape(TOK, 2 * C), ((0, ROWS - TOK), (0, 0)))
    weight = merge_weight.reshape(8, C, 2 * C)

    ahead = sent_back(
        (tokens[:SHIFT, SHIFT:], tokens[SHIFT:, :SHIFT], tokens[:SHIFT, :SHIFT])
    )
    weights = (scaled, turned, proj_weight, gather, scatter, codes, masks)
    first, *saved_first = forward_call(edges, tokens, (), weights, 1)
    rest, slab_d, slab_h, slab_dh, *saved_rest = forward_call(
        edges, tokens, ahead, weights, 3
    )
    high, low, main, left, *slabs = merge_call(
        tokens,
        first,
        rest,
        sent_on((slab_d, slab_h, slab_dh)),
        cot_rows,
        weight,
        parity,
    )
    ahead = sent_back(slabs)
    tables = (qkv_weight, wproj_wide, gather, scatter, masks, spread)
    sums = [struct((C, 3 * C), F32), struct((C, C), F32)]
    first, qkv_sum, proj_sum = backward_call(
        backward_first, "window_backward_first", high, (), saved_first, 0, tables, (), 1, sums, ()
    )
    main = block_sum(main)
    middle, qkv_sum, proj_sum = backward_call(
        backward_middle,
        "window_backward_middle",
        high,
        ahead,
        saved_rest,
        0,
        tables,
        (qkv_sum, proj_sum),
        2,
        sums,
        (),
        main,
    )
    main = block_spread(main)
    last, late = backward_call(
        backward_last,
        "window_backward_last",
        high,
        ahead,
        saved_rest,
        2,
        tables,
        (qkv_sum, proj_sum, left),
        1,
        [struct((LATE, TILE), BF)],
        [pltpu.VMEM((C, 3 * C), F32), pltpu.VMEM((C, C), F32)],
        main,
    )
    split_at = KEEP - WIN
    slabs = (
        jnp.concatenate([middle[1][split_at:], last[0][split_at:, :split_at]], axis=1),
        jnp.concatenate([middle[0][:, split_at:], last[0][:split_at, split_at:]], axis=0),
        last[0][split_at:, split_at:],
    )
    behind = sent_on(slabs)
    late = block_sum(late)
    token_grad = final_call(tokens, high, low, first, middle, last, behind, late)
    late = block_spread(late)
    merge_grad = jnp.concatenate([main, jnp.zeros((REST, TILE), BF)], axis=0).astype(F32)
    merge_grad = merge_grad.reshape(3, 8 * C, TILE).transpose(1, 0, 2).reshape(8 * C, 2 * C)
    end = late[TILES * C : TILES * C + REST].astype(F32)
    merge_grad = lax.dynamic_update_slice(merge_grad, end, (8 * C - REST, 2 * TILE))
    late = late[: TILES * C].reshape(TILES, C, TILE).transpose(1, 0, 2).reshape(C, 4 * C)
    late = late.astype(F32)
    return token_grad, late[:, : 3 * C], late[:, 3 * C :], merge_grad


def solution(mesh):
    placed = (P("gx", "gy", None, None), P(), P(), P(), P("gx", "gy", None, None))
    return jax.shard_map(
        local,
        mesh=mesh,
        in_specs=placed,
        out_specs=(P("gx", "gy", None, None), P(), P(), P()),
        check_vma=False,
    )
```

```python
import jax
import jax.numpy as jnp
import numpy as np
from jax import lax
from jax.experimental import pallas as pl
from jax.experimental.pallas import tpu as pltpu
from jax.sharding import PartitionSpec as P

C = 192
HEADS = 12
HD = 16
WIN = 7
SHIFT = 3
SIDE = 14
WPAD = 16
TOK = WIN**3
ROWS = 352
LROWS = 384
WIDE = 256
GROUP = WIN * WIN * WPAD
TILE = 128
CHUNK = 16
SPAN = CHUNK * WIN
FULL = WIN * WIN // CHUNK
TILES = 6
MAIN = 4608
LATE = 6144
STAT = 192
LABEL = 228
CLASSES = 8
FAR = 1e30
EPSILON = 1e-05
BF = jnp.bfloat16
F32 = jnp.float32
VMEM_LIMIT = 40 * 2**20


def head_masks():
    mask = np.zeros((HEADS, WIDE), np.float32)
    for head in range(HEADS):
        mask[head, head * HD : (head + 1) * HD] = 1
        for part in range(3):
            mask[head, STAT + part * HEADS + head] = 1
        mask[head, LABEL : LABEL + CLASSES] = 1
    return mask


def head_spread():
    spread = np.zeros((WIDE, WIDE), np.float32)
    for head in range(HEADS):
        for part in range(3):
            spread[head * HD : (head + 1) * HD, STAT + part * HEADS + head] = 1
    return spread


def group_table(width_of):
    table = np.zeros((2, CHUNK * WIN, CHUNK * WPAD), np.float32)
    for half in range(2):
        for pair in range(CHUNK):
            for place in range(WIN):
                table[half, pair * WIN + place, pair * WPAD + width_of(half, place)] = 1
    return table.reshape(2 * CHUNK * WIN, CHUNK * WPAD)


def window_table():
    return group_table(lambda half, place: (half * WIN + place + SHIFT) % SIDE)


def parity_table():
    return group_table(lambda parity, place: 2 * place + parity)


def class_codes():
    codes = np.full((LROWS, 1), CLASSES, np.int32)
    for place in range(TOK):
        i, j, k = place // (WIN * WIN), place // WIN % WIN, place % WIN
        codes[place, 0] = 4 * (i >= 4) + 2 * (j >= 4) + (k >= 4)
    return codes


def dot(a, b):
    return lax.dot_general(a, b, (((1,), (0,)), ((), ())), preferred_element_type=F32)


def dot_nt(a, b):
    return lax.dot_general(a, b, (((1,), (1,)), ((), ())), preferred_element_type=F32)


def dot_tn(a, b):
    return lax.dot_general(a, b, (((0,), (0,)), ((), ())), preferred_element_type=F32)


def gather_groups(table, block):
    halves = ([], [])
    for chunk in range(FULL):
        start = chunk * CHUNK * WPAD
        both = dot(table[...], block[start : start + CHUNK * WPAD])
        for half in range(2):
            halves[half].append(both[half * SPAN : (half + 1) * SPAN])
    tail = jnp.concatenate([table[:WPAD, :TILE], table[SPAN : SPAN + WPAD, :TILE]], axis=0)
    end = block[FULL * CHUNK * WPAD :]
    end = jnp.concatenate([end, jnp.zeros((TILE - WPAD, end.shape[1]), end.dtype)], axis=0)
    both = dot(tail, end)
    for half in range(2):
        halves[half].append(both[half * WPAD : (half + 1) * WPAD])
    return [jnp.concatenate(rows, axis=0) for rows in halves]


def scatter_groups(table, halves):
    out = []
    for chunk in range(FULL):
        rows = slice(chunk * SPAN, (chunk + 1) * SPAN)
        out.append(dot(table[...], jnp.concatenate([h[rows] for h in halves], axis=0)))
    pad = jnp.zeros((SPAN - WPAD, halves[0].shape[1]), halves[0].dtype)
    tail = [part for h in halves for part in (h[FULL * SPAN :], pad)]
    out.append(dot(table[:WPAD, :], jnp.concatenate(tail, axis=0)))
    return jnp.concatenate(out, axis=0)


def three_parts(value):
    high = value.astype(BF)
    rest = value - high.astype(F32)
    middle = rest.astype(BF)
    low = (rest - middle.astype(F32)).astype(BF)
    return high, middle, low


def dot_exact(value, table):
    high, middle, low = three_parts(value)
    return dot(high, table) + dot(middle, table) + dot(low, table)


def stat_lanes(value, lane):
    high, middle, low = three_parts(value)
    mixed = jnp.where(
        lane < STAT + HEADS,
        high.astype(F32),
        jnp.where(lane < STAT + 2 * HEADS, middle.astype(F32), low.astype(F32)),
    )
    return jnp.where((lane >= STAT) & (lane < STAT + 3 * HEADS), mixed, 0.0)


def norm_rows(values):
    centre = values - jnp.mean(values, axis=-1, keepdims=True)
    inv_std = lax.rsqrt(jnp.mean(centre * centre, axis=-1, keepdims=True) + EPSILON)
    return (centre * inv_std, inv_std)


def place_rolled(rolled, own, ahead_d, ahead_h, ahead_dh):
    keep = SIDE - SHIFT
    rolled[:, :, SIDE:, :] = jnp.zeros((SIDE, SIDE, WPAD - SIDE, C), rolled.dtype)
    rolled[0:keep, 0:keep, 0:SIDE, :] = own[SHIFT:, SHIFT:, :, :]
    rolled[keep:, 0:keep, 0:SIDE, :] = ahead_d[...]
    rolled[0:keep, keep:, 0:SIDE, :] = ahead_h[...]
    rolled[keep:, keep:, 0:SIDE, :] = ahead_dh[...]


def pair_corner(pair):
    return WIN * lax.div(pair, 2), WIN * lax.rem(pair, 2)


def forward_pair(
    wd,
    wh,
    block,
    edges,
    wqkv,
    wturned,
    wproj,
    gather,
    scatter,
    codes,
    masks,
    rows_out,
    q_out,
    k_out,
    kt_out,
    v_out,
    mixed_out,
    mixed_t,
    stat_t,
):
    lane = lax.broadcasted_iota(jnp.int32, (1, WIDE), 1)
    in_labels = (lane >= LABEL) & (lane < LABEL + CLASSES)
    in_stats = (lane >= STAT) & (lane < STAT + 3 * HEADS)
    normed, _ = norm_rows(block.reshape(GROUP, C).astype(F32))
    pad = jnp.zeros((LROWS - ROWS, C), BF)
    both = gather_groups(gather, normed.astype(BF))
    halves = []
    for half in range(2):
        rows = jnp.concatenate([both[half].astype(BF), pad], axis=0)
        rows_out[half] = rows[:ROWS]
        q = dot(rows, wqkv[0])
        k = dot(rows, wqkv[1])
        v = dot(rows, wqkv[2])
        kt_out[half] = dot_nt(wturned[0], rows).astype(BF)[:, :ROWS]
        vt = dot_nt(wturned[1], rows).astype(BF)[:, :ROWS]
        allowed = (
            4 * jnp.where(wd == 1, edges[0], 0)
            + 2 * jnp.where(wh == 1, edges[1], 0)
            + half
            + CLASSES
        )
        here = lane == LABEL + (codes[...] & allowed)
        q_aug = jnp.where(in_labels, jnp.where(here, 1.0, 0.0), q).astype(BF)
        k_aug = jnp.where(
            in_labels, jnp.where(here, 0.0, -FAR), jnp.where(in_stats, -1.0, k)
        ).astype(BF)[:ROWS]
        v_aug = jnp.where(in_stats, -1.0, v).astype(BF)[:ROWS]
        stat_t[half] = jnp.zeros((WIDE - TILE, LROWS), F32)
        for two in range(HEADS // 2):
            q_m = jnp.concatenate(
                [q_aug * masks[h : h + 1, :] for h in (2 * two, 2 * two + 1)], axis=0
            )
            scores = dot_nt(k_aug, q_m)
            top = jnp.max(scores, axis=0, keepdims=True)
            expo = jnp.exp(scores - top)
            sums = jnp.sum(expo, axis=0, keepdims=True)
            probs = (expo * (1.0 / sums)).astype(BF)
            stats = top + jnp.log(sums)
            mixed = dot(vt[2 * HD * two : 2 * HD * (two + 1)], probs)
            for i in range(2):
                h = 2 * two + i
                lanes = slice(i * LROWS, (i + 1) * LROWS)
                mixed_t[half, h * HD : (h + 1) * HD, :] = mixed[i * HD : (i + 1) * HD, lanes]
                for part in range(3):
                    row = STAT - TILE + part * HEADS + h
                    stat_t[half, row : row + 1, :] = stats[:, lanes]
        mixed = mixed_t[half].T[:ROWS]
        mixed_out[half] = mixed
        q_out[half, :, :TILE] = q_aug[:, :TILE]
        stats = stat_lanes(stat_t[half].T, lane[:, TILE:])
        q_out[half, :, TILE:] = (q_aug[:, TILE:].astype(F32) + stats).astype(BF)
        k_out[half] = k_aug
        v_out[half] = v_aug
        halves.append(dot(mixed.astype(BF), wproj[...]).astype(BF))
    back = scatter_groups(scatter, halves).astype(BF)
    return back.reshape(WIN, WIN, WPAD, C)[:, :, :SIDE, :]


def first_block(block, own):
    block[:, :, SIDE:, :] = jnp.zeros((WIN, WIN, WPAD - SIDE, C), BF)
    block[:, :, 0:SIDE, :] = own[SHIFT : SHIFT + WIN, SHIFT : SHIFT + WIN, :, :]
    return block[...]


def forward_first(edges, own, *refs):
    *weights, out, rows, q, k, kt, v, mixed, block, mixed_t, stat_t = refs
    out[0] = forward_pair(
        0, 0, first_block(block, own), edges, *weights, rows, q, k, kt, v, mixed, mixed_t, stat_t
    )


def forward_rest(edges, own, ahead_d, ahead_h, ahead_dh, *refs):
    (
        *weights,
        out,
        slab_d,
        slab_h,
        slab_dh,
        rows,
        q,
        k,
        kt,
        v,
        mixed,
        rolled,
        mixed_t,
        stat_t,
    ) = refs
    pair = pl.program_id(0) + 1

    @pl.when(pair == 1)
    def _():
        place_rolled(rolled, own, ahead_d, ahead_h, ahead_dh)

    at_d, at_h = pair_corner(pair)
    block = rolled[pl.ds(at_d, WIN), pl.ds(at_h, WIN), :, :]
    out[0] = forward_pair(
        lax.div(pair, 2),
        lax.rem(pair, 2),
        block,
        edges,
        *weights,
        rows,
        q,
        k,
        kt,
        v,
        mixed,
        mixed_t,
        stat_t,
    )
    split = KEEP - WIN

    @pl.when(pair == 1)
    def _():
        slab_h[0:WIN] = out[0, :, split:]

    @pl.when(pair == 2)
    def _():
        slab_d[:, 0:WIN] = out[0, split:]

    @pl.when(pair == 3)
    def _():
        slab_h[WIN:] = out[0, :split, split:]
        slab_d[:, WIN:] = out[0, split:, :split]
        slab_dh[...] = out[0, split:, split:]


def backward_pair(
    block,
    rows_in,
    q_in,
    k_in,
    kt_in,
    v_in,
    mixed_in,
    wqkv,
    wproj,
    gather,
    scatter,
    masks,
    spread,
    qkv_sum,
    proj_sum,
    grad_t,
):
    lane = lax.broadcasted_iota(jnp.int32, (1, WIDE), 1)
    pad = jnp.zeros((LROWS - ROWS, C), BF)
    both = gather_groups(gather, block.reshape(GROUP, C))
    halves = []
    for half in range(2):
        grads = jnp.concatenate([both[half].astype(BF), pad], axis=0)
        mixed = mixed_in[half]
        proj_sum[...] += dot_tn(mixed.astype(BF), grads[:ROWS])
        grad_o = dot_nt(grads, wproj[...]).astype(BF)
        delta = dot_exact(mixed * grad_o[:ROWS, :C].astype(F32), spread[...])
        delta = jnp.concatenate(
            [stat_lanes(delta, lane), jnp.zeros((LROWS - ROWS, WIDE), F32)], axis=0
        )
        o_aug = (grad_o.astype(F32) + delta).astype(BF)
        q_aug = q_in[half]
        k_aug = k_in[half]
        v_aug = v_in[half]
        grad_k = jnp.zeros((ROWS, WIDE), F32)
        grad_v = jnp.zeros((ROWS, WIDE), F32)
        for two in range(HEADS // 2):
            heads = (2 * two, 2 * two + 1)
            q_m = jnp.concatenate([q_aug * masks[h : h + 1, :] for h in heads], axis=0)
            o_m = jnp.concatenate([o_aug * masks[h : h + 1, :] for h in heads], axis=0)
            probs = jnp.exp(dot_nt(k_aug, q_m))
            slopes = (probs * dot_nt(v_aug, o_m)).astype(BF)
            grad_v = grad_v + dot(probs.astype(BF), o_m)
            grad_k = grad_k + dot(slopes, q_m)
            turned = dot(kt_in[half, 2 * HD * two : 2 * HD * (two + 1), :], slopes)
            for i, h in enumerate(heads):
                grad_t[half, h * HD : (h + 1) * HD, :] = turned[
                    i * HD : (i + 1) * HD, i * LROWS : (i + 1) * LROWS
                ]
        grad_q = (grad_t[half].T[:ROWS] * HD**-0.5).astype(BF)
        grad = jnp.concatenate(
            [grad_q, grad_k[:, :C].astype(BF), grad_v[:, :C].astype(BF)], axis=1
        )
        qkv_sum[...] += dot_tn(rows_in[half], grad)
        halves.append(dot_nt(grad, wqkv[...]).astype(BF))
    back = scatter_groups(scatter, halves).astype(BF)
    return back.reshape(WIN, WIN, WPAD, C)[:, :, :SIDE, :]


def backward_first(own, *refs):
    *inputs, out, qkv_sum, proj_sum, block, grad_t = refs
    qkv_sum[...] = jnp.zeros_like(qkv_sum)
    proj_sum[...] = jnp.zeros_like(proj_sum)
    out[0] = backward_pair(first_block(block, own), *inputs, qkv_sum, proj_sum, grad_t)


def backward_rest(own, ahead_d, ahead_h, ahead_dh, *refs):
    *inputs, qkv_in, proj_in, main, out, late, rolled, grad_t, qkv_sum, proj_sum = refs
    pair = pl.program_id(0) + 1

    @pl.when(pair == 1)
    def _():
        place_rolled(rolled, own, ahead_d, ahead_h, ahead_dh)
        qkv_sum[...] = qkv_in[...]
        proj_sum[...] = proj_in[...]
        late[0:MAIN, :] = main[...]
        late[MAIN + TILES * C :, :] = jnp.zeros((LATE - MAIN - TILES * C, TILE), BF)

    at_d, at_h = pair_corner(pair)
    block = rolled[pl.ds(at_d, WIN), pl.ds(at_h, WIN), :, :]
    out[0] = backward_pair(block, *inputs, qkv_sum, proj_sum, grad_t)

    @pl.when(pair == 3)
    def _():
        table = jnp.concatenate([qkv_sum[...], proj_sum[...]], axis=1).astype(BF)
        for tile in range(TILES):
            start = MAIN + tile * C
            late[start : start + C, :] = table[:, tile * TILE : (tile + 1) * TILE]


def unpack_kernel(late, qkv_out, proj_out, merge_out):
    for tile in range(3):
        rows = late[tile * 8 * C : (tile + 1) * 8 * C, :]
        merge_out[:, tile * TILE : (tile + 1) * TILE] = rows.astype(F32)
    table = jnp.concatenate(
        [late[MAIN + tile * C : MAIN + (tile + 1) * C, :].astype(F32) for tile in range(TILES)],
        axis=1,
    )
    qkv_out[...] = table[:, : 3 * C]
    proj_out[...] = table[:, 3 * C :]


def whole(shape):
    return pl.BlockSpec(shape, lambda step: (0,) * len(shape))


def per_pair(shape, first=0):
    return pl.BlockSpec(shape, lambda step: (step + first,) + (0,) * (len(shape) - 1))


KEEP = SIDE - SHIFT
GRID = (SIDE, SIDE, SIDE, C)
SLABS = ((SHIFT, KEEP, SIDE, C), (KEEP, SHIFT, SIDE, C), (SHIFT, SHIFT, SIDE, C))
SAVED = (
    ((ROWS, C), BF),
    ((LROWS, WIDE), BF),
    ((ROWS, WIDE), BF),
    ((C, ROWS), BF),
    ((ROWS, WIDE), BF),
    ((ROWS, C), F32),
)
PAIR = (1, WIN, WIN, SIDE, C)


def struct(shape, dtype):
    return jax.ShapeDtypeStruct(shape, dtype)


def call(kernel, name, count, operands, in_specs, outs, scratch, gigaflops):
    return pl.pallas_call(
        kernel,
        grid=(count,),
        in_specs=in_specs,
        out_specs=[spec for spec, _ in outs],
        out_shape=[shape for _, shape in outs],
        scratch_shapes=scratch,
        compiler_params=pltpu.CompilerParams(
            dimension_semantics=("arbitrary",), vmem_limit_bytes=VMEM_LIMIT
        ),
        cost_estimate=pl.CostEstimate(
            flops=int(gigaflops * 1e9), bytes_accessed=8 * 2**20, transcendentals=0
        ),
        name=name,
    )(*operands)


def in_hbm(array):
    return pltpu.with_memory_space_constraint(array, pltpu.HBM)


def whole_specs(arrays):
    return [whole(a.shape) for a in arrays]


def forward_call(edges, grid, slabs, weights, count):
    saved = [
        (per_pair((2,) + shape), pltpu.HBM((2 * count,) + shape, dtype))
        for shape, dtype in SAVED
    ]
    out = [(per_pair(PAIR), struct((count,) + PAIR[1:], BF))]
    scratch = [pltpu.VMEM((2, C, LROWS), F32), pltpu.VMEM((2, WIDE - TILE, LROWS), F32)]
    if slabs:
        out += [(whole(s), struct(s, BF)) for s in SLABS]
        scratch = [pltpu.VMEM((SIDE, SIDE, WPAD, C), BF)] + scratch
    else:
        scratch = [pltpu.VMEM((WIN, WIN, WPAD, C), BF)] + scratch
    operands = [grid, *slabs, *weights]
    return call(
        forward_rest if slabs else forward_first,
        "window_forward_rest" if slabs else "window_forward_first",
        count,
        [edges] + operands,
        [pl.BlockSpec(memory_space=pltpu.SMEM)] + whole_specs(operands),
        out + saved,
        scratch,
        5.0 * count,
    )


def backward_call(kernel, name, grid, slabs, saved, skip, tables, extra, count, outs, scratch):
    lead = [grid, *slabs]
    specs = whole_specs(lead)
    specs += [per_pair((2,) + shape, skip) for shape, _ in SAVED]
    specs += whole_specs([*tables, *extra])
    side = SIDE if slabs else WIN
    scratch = [
        pltpu.VMEM((side, side, WPAD, C), BF),
        pltpu.VMEM((2, C, LROWS), F32),
        *scratch,
    ]
    outs = [(per_pair(PAIR), struct((count,) + PAIR[1:], BF))] + [
        (whole(o.shape), o) for o in outs
    ]
    operands = [*lead, *[in_hbm(s) for s in saved], *tables, *extra]
    return call(kernel, name, count, operands, specs, outs, scratch, 12.0 * count)


def place_trailing(target, first, rest, behind_d, behind_h, behind_dh):
    split = KEEP - WIN
    target[SHIFT : SHIFT + WIN, SHIFT : SHIFT + WIN, 0:SIDE, :] = first[0]
    target[SHIFT : SHIFT + WIN, SHIFT + WIN :, 0:SIDE, :] = rest[0][:, :split]
    target[SHIFT + WIN :, SHIFT : SHIFT + WIN, 0:SIDE, :] = rest[1][:split]
    target[SHIFT + WIN :, SHIFT + WIN :, 0:SIDE, :] = rest[2][:split, :split]
    target[0:SHIFT, SHIFT:, 0:SIDE, :] = behind_d[...]
    target[SHIFT:, 0:SHIFT, 0:SIDE, :] = behind_h[...]
    target[0:SHIFT, 0:SHIFT, 0:SIDE, :] = behind_dh[...]


def merge_kernel(
    tokens,
    first,
    rest,
    behind_d,
    behind_h,
    behind_dh,
    cotangent,
    weight,
    gather,
    scatter,
    high_out,
    low_out,
    main_out,
    slab_d,
    slab_h,
    slab_dh,
    block,
    pieces,
):
    block[:, :, SIDE:, :] = jnp.zeros((SIDE, SIDE, WPAD - SIDE, C), BF)
    place_trailing(block, first, rest, behind_d, behind_h, behind_dh)
    block[:, :, 0:SIDE, :] = (
        tokens[...].astype(F32) + block[:, :, 0:SIDE, :].astype(F32)
    ).astype(BF)
    total = jnp.zeros((ROWS, 1), F32)
    for pair in range(4):
        a, b = pair // 2, pair % 2
        part = block[...].reshape(WIN, 2, WIN, 2, WPAD, C)[:, a, :, b]
        both = gather_groups(gather, part.reshape(GROUP, C))
        for c in range(2):
            piece = both[c]
            pieces[2 * pair + c] = piece
            total = total + jnp.sum(piece, axis=-1, keepdims=True)
    mean = total / (8 * C)
    square = jnp.zeros((ROWS, 1), F32)
    for index in range(8):
        centre = pieces[index] - mean
        square = square + jnp.sum(centre * centre, axis=-1, keepdims=True)
    inv_std = lax.rsqrt(square / (8 * C) + EPSILON)
    grad_sum = jnp.zeros((ROWS, 1), F32)
    cross_sum = jnp.zeros((ROWS, 1), F32)
    cot = cotangent[...]
    for index in range(8):
        normed = (pieces[index] - mean) * inv_std
        part = dot_tn(normed.astype(BF), cot).astype(BF)
        for tile in range(3):
            start = (tile * 8 + index) * C
            main_out[start : start + C, :] = part[:, tile * TILE : (tile + 1) * TILE]
        grad = dot_nt(cot, weight[index])
        grad_sum = grad_sum + jnp.sum(grad, axis=-1, keepdims=True)
        cross_sum = cross_sum + jnp.sum(grad * normed, axis=-1, keepdims=True)
    grad_mean = grad_sum / (8 * C)
    cross_mean = cross_sum / (8 * C)
    for a in range(2):
        highs, lows = [], []
        for b in range(2):
            high_pair, low_pair = [], []
            for c in range(2):
                index = 4 * a + 2 * b + c
                normed = (pieces[index] - mean) * inv_std
                grad = dot_nt(cot, weight[index])
                grad = inv_std * (grad - grad_mean - normed * cross_mean)
                high = grad.astype(BF)
                high_pair.append(high)
                low_pair.append((grad - high.astype(F32)).astype(BF))
            for pair, kept in ((high_pair, highs), (low_pair, lows)):
                laid = scatter_groups(scatter, pair).astype(BF)
                kept.append(laid.reshape(WIN, WIN, WPAD, C))
        for kept, out in ((highs, high_out), (lows, low_out)):
            merged = jnp.stack(kept, axis=2).reshape(WIN, SIDE, WPAD, C)
            for i in range(WIN):
                out[2 * i + a] = merged[i, :, :SIDE, :]
    slab_d[...] = high_out[:SHIFT, SHIFT:]
    slab_h[...] = high_out[SHIFT:, :SHIFT]
    slab_dh[...] = high_out[:SHIFT, :SHIFT]


def final_kernel(
    tokens, high, low, first, rest, behind_d, behind_h, behind_dh, _, out, grads
):
    place_trailing(grads, first, rest, behind_d, behind_h, behind_dh)

    @pl.loop(0, SIDE)
    def row(d):
        normed, inv_std = norm_rows(tokens[d].astype(F32))
        grad = grads[d].astype(F32)
        back = inv_std * (
            grad
            - jnp.mean(grad, axis=-1, keepdims=True)
            - normed * jnp.mean(grad * normed, axis=-1, keepdims=True)
        )
        out[d] = (high[d].astype(F32) + low[d].astype(F32) + back).astype(BF)


def merge_call(tokens, first, rest, slabs, cot_rows, weight, parity):
    operands = [in_hbm(tokens), first, rest, *slabs, cot_rows, in_hbm(weight), *parity]
    shapes = [GRID, GRID, (MAIN, TILE), *SLABS]
    kinds = [struct, pltpu.HBM, pltpu.HBM, struct, struct, struct]
    return call(
        merge_kernel,
        "merge_backward",
        1,
        operands,
        whole_specs(operands),
        [(whole(s), kind(s, BF)) for s, kind in zip(shapes, kinds)],
        [pltpu.VMEM((SIDE, SIDE, WPAD, C), BF), pltpu.VMEM((8, ROWS, C), F32)],
        10.0,
    )


def final_call(tokens, high, low, first, rest, slabs, after):
    operands = [in_hbm(tokens), in_hbm(high), in_hbm(low), first, rest, *slabs]
    return call(
        final_kernel,
        "token_gradient",
        1,
        operands + [after],
        whole_specs(operands) + [pl.BlockSpec(memory_space=pl.ANY)],
        [(whole(GRID), struct(GRID, BF))],
        [pltpu.VMEM(GRID, BF)],
        7.0,
    )[0]


def moved(value, steps_d, steps_h):
    count_d, count_h = lax.axis_size("gx"), lax.axis_size("gy")
    pairs = []
    for d in range(count_d):
        for h in range(count_h):
            target = (d + steps_d) % count_d * count_h + (h + steps_h) % count_h
            pairs.append((d * count_h + h, target))
    return lax.ppermute(value, ("gx", "gy"), pairs)


def sent_back(slabs):
    d, h, dh = slabs
    return moved(d, -1, 0), moved(h, 0, -1), moved(dh, -1, -1)


def sent_on(slabs):
    d, h, dh = slabs
    return moved(d, 1, 0), moved(h, 0, 1), moved(dh, 1, 1)


def exchanged(blocks):
    return lax.all_to_all(blocks, ("gx", "gy"), 0, 0, tiled=True)


def block_sum(part):
    count = lax.axis_size(("gx", "gy"))
    blocks = exchanged(part.reshape(count, part.shape[0] // count, TILE))
    return jnp.sum(blocks.astype(F32), axis=0).astype(BF)


def block_spread(own):
    count = lax.axis_size(("gx", "gy"))
    spread = exchanged(jnp.broadcast_to(own[None], (count,) + own.shape))
    return spread.reshape(count * own.shape[0], TILE)


def local(tokens, qkv_weight, proj_weight, merge_weight, cotangent):
    gather = jnp.asarray(window_table(), BF)
    scatter = jnp.asarray(window_table().T, BF)
    parity = (jnp.asarray(parity_table(), BF), jnp.asarray(parity_table().T, BF))
    codes = jnp.asarray(class_codes())
    masks = jnp.asarray(head_masks(), BF)
    spread = jnp.asarray(head_spread()[:C], BF)
    edges = jnp.stack(
        [
            (lax.axis_index("gx") == lax.axis_size("gx") - 1).astype(jnp.int32),
            (lax.axis_index("gy") == lax.axis_size("gy") - 1).astype(jnp.int32),
        ]
    )
    split = qkv_weight.reshape(C, 3, C).transpose(1, 0, 2)
    scaled = jnp.concatenate([split[:1] * BF(HD**-0.5), split[1:]], axis=0)
    scaled = jnp.pad(scaled, ((0, 0), (0, 0), (0, WIDE - C)))
    turned = split[1:].transpose(0, 2, 1)
    wproj_wide = jnp.pad(proj_weight, ((0, WIDE - C), (0, 0)))
    cot_rows = jnp.pad(cotangent.reshape(TOK, 2 * C), ((0, ROWS - TOK), (0, 0)))
    weight = merge_weight.reshape(8, C, 2 * C)

    ahead = sent_back(
        (tokens[:SHIFT, SHIFT:], tokens[SHIFT:, :SHIFT], tokens[:SHIFT, :SHIFT])
    )
    weights = (scaled, turned, proj_weight, gather, scatter, codes, masks)
    first, *saved_first = forward_call(edges, tokens, (), weights, 1)
    rest, slab_d, slab_h, slab_dh, *saved_rest = forward_call(
        edges, tokens, ahead, weights, 3
    )
    high, low, main, *slabs = merge_call(
        tokens,
        first,
        rest,
        sent_on((slab_d, slab_h, slab_dh)),
        cot_rows,
        weight,
        parity,
    )
    ahead = sent_back(slabs)
    tables = (qkv_weight, wproj_wide, gather, scatter, masks, spread)
    sums = [struct((C, 3 * C), F32), struct((C, C), F32)]
    first, qkv_sum, proj_sum = backward_call(
        backward_first, "window_backward_first", high, (), saved_first, 0, tables, (), 1, sums, ()
    )
    rest, late = backward_call(
        backward_rest,
        "window_backward_rest",
        high,
        ahead,
        saved_rest,
        0,
        tables,
        (qkv_sum, proj_sum, in_hbm(main)),
        3,
        [struct((LATE, TILE), BF)],
        [pltpu.VMEM((C, 3 * C), F32), pltpu.VMEM((C, C), F32)],
    )
    at = KEEP - WIN
    slabs = (
        jnp.concatenate([rest[1][at:], rest[2][at:, :at]], axis=1),
        jnp.concatenate([rest[0][:, at:], rest[2][:at, at:]], axis=0),
        rest[2][at:, at:],
    )
    behind = sent_on(slabs)
    late, *behind = lax.optimization_barrier((block_sum(late), *behind))
    token_grad = final_call(tokens, high, low, first, rest, behind, late)
    late = block_spread(late)
    shapes = [(C, 3 * C), (C, C), (8 * C, 2 * C)]
    weight_grads = call(
        unpack_kernel,
        "unpack",
        1,
        [late],
        whole_specs([late]),
        [(whole(s), struct(s, F32)) for s in shapes],
        [],
        1.0,
    )
    return (token_grad, *weight_grads)


def solution(mesh):
    placed = (P("gx", "gy", None, None), P(), P(), P(), P("gx", "gy", None, None))
    return jax.shard_map(
        local,
        mesh=mesh,
        in_specs=placed,
        out_specs=(P("gx", "gy", None, None), P(), P(), P()),
        check_vma=False,
    )
```

```python
import jax
import jax.numpy as jnp
import numpy as np
from jax import lax
from jax.experimental import pallas as pl
from jax.experimental.pallas import tpu as pltpu
from jax.sharding import PartitionSpec as P

C = 192
HEADS = 12
HD = 16
WIN = 7
SHIFT = 3
SIDE = 14
WPAD = 16
TOK = WIN**3
ROWS = 352
LROWS = 384
WIDE = 256
GROUP = WIN * WIN * WPAD
TILE = 128
CHUNK = 16
SPAN = CHUNK * WIN
FULL = WIN * WIN // CHUNK
TILES = 6
MAIN = 4608
LATE = 6144
HALF = LATE // 2
STAT = 192
LABEL = 228
CLASSES = 8
FAR = 1e30
EPSILON = 1e-05
BF = jnp.bfloat16
F32 = jnp.float32
VMEM_LIMIT = 40 * 2**20


def head_masks():
    mask = np.zeros((HEADS, WIDE), np.float32)
    for head in range(HEADS):
        mask[head, head * HD : (head + 1) * HD] = 1
        for part in range(3):
            mask[head, STAT + part * HEADS + head] = 1
        mask[head, LABEL : LABEL + CLASSES] = 1
    return mask


def head_spread():
    spread = np.zeros((WIDE, WIDE), np.float32)
    for head in range(HEADS):
        for part in range(3):
            spread[head * HD : (head + 1) * HD, STAT + part * HEADS + head] = 1
    return spread


def group_table(width_of):
    table = np.zeros((2, CHUNK * WIN, CHUNK * WPAD), np.float32)
    for half in range(2):
        for pair in range(CHUNK):
            for place in range(WIN):
                table[half, pair * WIN + place, pair * WPAD + width_of(half, place)] = 1
    return table.reshape(2 * CHUNK * WIN, CHUNK * WPAD)


def window_table():
    return group_table(lambda half, place: (half * WIN + place + SHIFT) % SIDE)


def parity_table():
    return group_table(lambda parity, place: 2 * place + parity)


def class_codes():
    codes = np.full((LROWS, 1), CLASSES, np.int32)
    for place in range(TOK):
        i, j, k = place // (WIN * WIN), place // WIN % WIN, place % WIN
        codes[place, 0] = 4 * (i >= 4) + 2 * (j >= 4) + (k >= 4)
    return codes


def dot(a, b):
    return lax.dot_general(a, b, (((1,), (0,)), ((), ())), preferred_element_type=F32)


def dot_nt(a, b):
    return lax.dot_general(a, b, (((1,), (1,)), ((), ())), preferred_element_type=F32)


def dot_tn(a, b):
    return lax.dot_general(a, b, (((0,), (0,)), ((), ())), preferred_element_type=F32)


def gather_groups(table, block):
    halves = ([], [])
    for chunk in range(FULL):
        start = chunk * CHUNK * WPAD
        both = dot(table[...], block[start : start + CHUNK * WPAD])
        for half in range(2):
            halves[half].append(both[half * SPAN : (half + 1) * SPAN])
    tail = jnp.concatenate([table[:WPAD, :TILE], table[SPAN : SPAN + WPAD, :TILE]], axis=0)
    end = block[FULL * CHUNK * WPAD :]
    end = jnp.concatenate([end, jnp.zeros((TILE - WPAD, end.shape[1]), end.dtype)], axis=0)
    both = dot(tail, end)
    for half in range(2):
        halves[half].append(both[half * WPAD : (half + 1) * WPAD])
    return [jnp.concatenate(rows, axis=0) for rows in halves]


def scatter_groups(table, halves):
    out = []
    for chunk in range(FULL):
        rows = slice(chunk * SPAN, (chunk + 1) * SPAN)
        out.append(dot(table[...], jnp.concatenate([h[rows] for h in halves], axis=0)))
    pad = jnp.zeros((SPAN - WPAD, halves[0].shape[1]), halves[0].dtype)
    tail = [part for h in halves for part in (h[FULL * SPAN :], pad)]
    out.append(dot(table[:WPAD, :], jnp.concatenate(tail, axis=0)))
    return jnp.concatenate(out, axis=0)


def three_parts(value):
    high = value.astype(BF)
    rest = value - high.astype(F32)
    middle = rest.astype(BF)
    low = (rest - middle.astype(F32)).astype(BF)
    return high, middle, low


def dot_exact(value, table):
    high, middle, low = three_parts(value)
    return dot(high, table) + dot(middle, table) + dot(low, table)


def stat_lanes(value, lane):
    high, middle, low = three_parts(value)
    mixed = jnp.where(
        lane < STAT + HEADS,
        high.astype(F32),
        jnp.where(lane < STAT + 2 * HEADS, middle.astype(F32), low.astype(F32)),
    )
    return jnp.where((lane >= STAT) & (lane < STAT + 3 * HEADS), mixed, 0.0)


def norm_rows(values):
    centre = values - jnp.mean(values, axis=-1, keepdims=True)
    inv_std = lax.rsqrt(jnp.mean(centre * centre, axis=-1, keepdims=True) + EPSILON)
    return (centre * inv_std, inv_std)


def place_rolled(rolled, own, ahead_d, ahead_h, ahead_dh):
    keep = SIDE - SHIFT
    rolled[:, :, SIDE:, :] = jnp.zeros((SIDE, SIDE, WPAD - SIDE, C), rolled.dtype)
    rolled[0:keep, 0:keep, 0:SIDE, :] = own[SHIFT:, SHIFT:, :, :]
    rolled[keep:, 0:keep, 0:SIDE, :] = ahead_d[...]
    rolled[0:keep, keep:, 0:SIDE, :] = ahead_h[...]
    rolled[keep:, keep:, 0:SIDE, :] = ahead_dh[...]


def pair_corner(pair):
    return WIN * lax.div(pair, 2), WIN * lax.rem(pair, 2)


def forward_pair(
    wd,
    wh,
    block,
    edges,
    wqkv,
    wturned,
    wproj,
    gather,
    scatter,
    codes,
    masks,
    rows_out,
    q_out,
    k_out,
    kt_out,
    v_out,
    mixed_out,
    mixed_t,
    stat_t,
):
    lane = lax.broadcasted_iota(jnp.int32, (1, WIDE), 1)
    in_labels = (lane >= LABEL) & (lane < LABEL + CLASSES)
    in_stats = (lane >= STAT) & (lane < STAT + 3 * HEADS)
    normed, _ = norm_rows(block.reshape(GROUP, C).astype(F32))
    pad = jnp.zeros((LROWS - ROWS, C), BF)
    both = gather_groups(gather, normed.astype(BF))
    halves = []
    for half in range(2):
        rows = jnp.concatenate([both[half].astype(BF), pad], axis=0)
        rows_out[half] = rows[:ROWS]
        q = dot(rows, wqkv[0])
        k = dot(rows, wqkv[1])
        v = dot(rows, wqkv[2])
        kt_out[half] = dot_nt(wturned[0], rows).astype(BF)[:, :ROWS]
        vt = dot_nt(wturned[1], rows).astype(BF)[:, :ROWS]
        allowed = (
            4 * jnp.where(wd == 1, edges[0], 0)
            + 2 * jnp.where(wh == 1, edges[1], 0)
            + half
            + CLASSES
        )
        here = lane == LABEL + (codes[...] & allowed)
        q_aug = jnp.where(in_labels, jnp.where(here, 1.0, 0.0), q).astype(BF)
        k_aug = jnp.where(
            in_labels, jnp.where(here, 0.0, -FAR), jnp.where(in_stats, -1.0, k)
        ).astype(BF)[:ROWS]
        v_aug = jnp.where(in_stats, -1.0, v).astype(BF)[:ROWS]
        stat_t[half] = jnp.zeros((WIDE - TILE, LROWS), F32)
        for two in range(HEADS // 2):
            q_m = jnp.concatenate(
                [q_aug * masks[h : h + 1, :] for h in (2 * two, 2 * two + 1)], axis=0
            )
            scores = dot_nt(k_aug, q_m)
            top = jnp.max(scores, axis=0, keepdims=True)
            expo = jnp.exp(scores - top)
            sums = jnp.sum(expo, axis=0, keepdims=True)
            probs = (expo * (1.0 / sums)).astype(BF)
            stats = top + jnp.log(sums)
            mixed = dot(vt[2 * HD * two : 2 * HD * (two + 1)], probs)
            for i in range(2):
                h = 2 * two + i
                lanes = slice(i * LROWS, (i + 1) * LROWS)
                mixed_t[half, h * HD : (h + 1) * HD, :] = mixed[i * HD : (i + 1) * HD, lanes]
                for part in range(3):
                    row = STAT - TILE + part * HEADS + h
                    stat_t[half, row : row + 1, :] = stats[:, lanes]
        mixed = mixed_t[half].T[:ROWS]
        mixed_out[half] = mixed
        q_out[half, :, :TILE] = q_aug[:, :TILE]
        stats = stat_lanes(stat_t[half].T, lane[:, TILE:])
        q_out[half, :, TILE:] = (q_aug[:, TILE:].astype(F32) + stats).astype(BF)
        k_out[half] = k_aug
        v_out[half] = v_aug
        halves.append(dot(mixed.astype(BF), wproj[...]).astype(BF))
    back = scatter_groups(scatter, halves).astype(BF)
    return back.reshape(WIN, WIN, WPAD, C)[:, :, :SIDE, :]


def first_block(block, own):
    block[:, :, SIDE:, :] = jnp.zeros((WIN, WIN, WPAD - SIDE, C), BF)
    block[:, :, 0:SIDE, :] = own[SHIFT : SHIFT + WIN, SHIFT : SHIFT + WIN, :, :]
    return block[...]


def forward_first(edges, own, *refs):
    *weights, out, rows, q, k, kt, v, mixed, block, mixed_t, stat_t = refs
    out[0] = forward_pair(
        0, 0, first_block(block, own), edges, *weights, rows, q, k, kt, v, mixed, mixed_t, stat_t
    )


def forward_rest(edges, own, ahead_d, ahead_h, ahead_dh, *refs):
    (
        *weights,
        out,
        slab_d,
        slab_h,
        slab_dh,
        rows,
        q,
        k,
        kt,
        v,
        mixed,
        rolled,
        mixed_t,
        stat_t,
    ) = refs
    pair = pl.program_id(0) + 1

    @pl.when(pair == 1)
    def _():
        place_rolled(rolled, own, ahead_d, ahead_h, ahead_dh)

    at_d, at_h = pair_corner(pair)
    block = rolled[pl.ds(at_d, WIN), pl.ds(at_h, WIN), :, :]
    out[0] = forward_pair(
        lax.div(pair, 2),
        lax.rem(pair, 2),
        block,
        edges,
        *weights,
        rows,
        q,
        k,
        kt,
        v,
        mixed,
        mixed_t,
        stat_t,
    )
    split = KEEP - WIN

    @pl.when(pair == 1)
    def _():
        slab_h[0:WIN] = out[0, :, split:]

    @pl.when(pair == 2)
    def _():
        slab_d[:, 0:WIN] = out[0, split:]

    @pl.when(pair == 3)
    def _():
        slab_h[WIN:] = out[0, :split, split:]
        slab_d[:, WIN:] = out[0, split:, :split]
        slab_dh[...] = out[0, split:, split:]


def backward_pair(
    block,
    rows_in,
    q_in,
    k_in,
    kt_in,
    v_in,
    mixed_in,
    wqkv,
    wproj,
    gather,
    scatter,
    masks,
    spread,
    qkv_sum,
    proj_sum,
    grad_t,
):
    lane = lax.broadcasted_iota(jnp.int32, (1, WIDE), 1)
    pad = jnp.zeros((LROWS - ROWS, C), BF)
    both = gather_groups(gather, block.reshape(GROUP, C))
    halves = []
    for half in range(2):
        grads = jnp.concatenate([both[half].astype(BF), pad], axis=0)
        mixed = mixed_in[half]
        proj_sum[...] += dot_tn(mixed.astype(BF), grads[:ROWS])
        grad_o = dot_nt(grads, wproj[...]).astype(BF)
        delta = dot_exact(mixed * grad_o[:ROWS, :C].astype(F32), spread[...])
        delta = jnp.concatenate(
            [stat_lanes(delta, lane), jnp.zeros((LROWS - ROWS, WIDE), F32)], axis=0
        )
        o_aug = (grad_o.astype(F32) + delta).astype(BF)
        q_aug = q_in[half]
        k_aug = k_in[half]
        v_aug = v_in[half]
        grad_k = jnp.zeros((ROWS, WIDE), F32)
        grad_v = jnp.zeros((ROWS, WIDE), F32)
        for two in range(HEADS // 2):
            heads = (2 * two, 2 * two + 1)
            q_m = jnp.concatenate([q_aug * masks[h : h + 1, :] for h in heads], axis=0)
            o_m = jnp.concatenate([o_aug * masks[h : h + 1, :] for h in heads], axis=0)
            probs = jnp.exp(dot_nt(k_aug, q_m))
            slopes = (probs * dot_nt(v_aug, o_m)).astype(BF)
            grad_v = grad_v + dot(probs.astype(BF), o_m)
            grad_k = grad_k + dot(slopes, q_m)
            turned = dot(kt_in[half, 2 * HD * two : 2 * HD * (two + 1), :], slopes)
            for i, h in enumerate(heads):
                grad_t[half, h * HD : (h + 1) * HD, :] = turned[
                    i * HD : (i + 1) * HD, i * LROWS : (i + 1) * LROWS
                ]
        grad_q = (grad_t[half].T[:ROWS] * HD**-0.5).astype(BF)
        grad = jnp.concatenate(
            [grad_q, grad_k[:, :C].astype(BF), grad_v[:, :C].astype(BF)], axis=1
        )
        qkv_sum[...] += dot_tn(rows_in[half], grad)
        halves.append(dot_nt(grad, wqkv[...]).astype(BF))
    back = scatter_groups(scatter, halves).astype(BF)
    return back.reshape(WIN, WIN, WPAD, C)[:, :, :SIDE, :]


def backward_first(own, *refs):
    *inputs, out, qkv_sum, proj_sum, block, grad_t = refs
    qkv_sum[...] = jnp.zeros_like(qkv_sum)
    proj_sum[...] = jnp.zeros_like(proj_sum)
    out[0] = backward_pair(first_block(block, own), *inputs, qkv_sum, proj_sum, grad_t)


def backward_rest(own, ahead_d, ahead_h, ahead_dh, *refs):
    (
        *inputs,
        qkv_in,
        proj_in,
        main,
        core,
        out,
        kept,
        given,
        rolled,
        grad_t,
        qkv_sum,
        proj_sum,
        late,
    ) = refs
    pair = pl.program_id(0) + 1

    @pl.when(pair == 1)
    def _():
        place_rolled(rolled, own, ahead_d, ahead_h, ahead_dh)
        qkv_sum[...] = qkv_in[...]
        proj_sum[...] = proj_in[...]
        late[0:MAIN, :] = main[...]
        late[MAIN + TILES * C :, :] = jnp.zeros((LATE - MAIN - TILES * C, TILE), BF)

    at_d, at_h = pair_corner(pair)
    block = rolled[pl.ds(at_d, WIN), pl.ds(at_h, WIN), :, :]
    out[0] = backward_pair(block, *inputs, qkv_sum, proj_sum, grad_t)

    @pl.when(pair == 3)
    def _():
        table = jnp.concatenate([qkv_sum[...], proj_sum[...]], axis=1).astype(BF)
        for tile in range(TILES):
            start = MAIN + tile * C
            late[start : start + C, :] = table[:, tile * TILE : (tile + 1) * TILE]
        kept[...] = late[pl.ds(core[0] * HALF, HALF), :]
        given[...] = late[pl.ds((1 - core[0]) * HALF, HALF), :]


def unpack_kernel(core, mine, other, qkv_out, proj_out, merge_out):
    first = core[0] == 0
    low = jnp.where(first, mine[...].astype(F32), other[...].astype(F32))
    high = jnp.where(first, other[...].astype(F32), mine[...].astype(F32))
    rows = 8 * C
    for tile, part in enumerate((low[:rows], low[rows:], high[:rows])):
        merge_out[:, tile * TILE : (tile + 1) * TILE] = part
    rest = high[rows:]
    table = jnp.concatenate(
        [rest[tile * C : (tile + 1) * C, :] for tile in range(TILES)], axis=1
    )
    qkv_out[...] = table[:, : 3 * C]
    proj_out[...] = table[:, 3 * C :]


def whole(shape):
    return pl.BlockSpec(shape, lambda step: (0,) * len(shape))


def per_pair(shape, first=0):
    return pl.BlockSpec(shape, lambda step: (step + first,) + (0,) * (len(shape) - 1))


KEEP = SIDE - SHIFT
GRID = (SIDE, SIDE, SIDE, C)
SLABS = ((SHIFT, KEEP, SIDE, C), (KEEP, SHIFT, SIDE, C), (SHIFT, SHIFT, SIDE, C))
SAVED = (
    ((ROWS, C), BF),
    ((LROWS, WIDE), BF),
    ((ROWS, WIDE), BF),
    ((C, ROWS), BF),
    ((ROWS, WIDE), BF),
    ((ROWS, C), F32),
)
PAIR = (1, WIN, WIN, SIDE, C)


def struct(shape, dtype):
    return jax.ShapeDtypeStruct(shape, dtype)


def call(kernel, name, count, operands, in_specs, outs, scratch, gigaflops):
    return pl.pallas_call(
        kernel,
        grid=(count,),
        in_specs=in_specs,
        out_specs=[spec for spec, _ in outs],
        out_shape=[shape for _, shape in outs],
        scratch_shapes=scratch,
        compiler_params=pltpu.CompilerParams(
            dimension_semantics=("arbitrary",), vmem_limit_bytes=VMEM_LIMIT
        ),
        cost_estimate=pl.CostEstimate(
            flops=int(gigaflops * 1e9), bytes_accessed=8 * 2**20, transcendentals=0
        ),
        name=name,
    )(*operands)


def in_hbm(array):
    return pltpu.with_memory_space_constraint(array, pltpu.HBM)


def whole_specs(arrays):
    return [whole(a.shape) for a in arrays]


def forward_call(edges, grid, slabs, weights, count):
    saved = [
        (per_pair((2,) + shape), pltpu.HBM((2 * count,) + shape, dtype))
        for shape, dtype in SAVED
    ]
    out = [(per_pair(PAIR), pltpu.HBM((count,) + PAIR[1:], BF))]
    scratch = [pltpu.VMEM((2, C, LROWS), F32), pltpu.VMEM((2, WIDE - TILE, LROWS), F32)]
    if slabs:
        out += [(whole(s), struct(s, BF)) for s in SLABS]
        scratch = [pltpu.VMEM((SIDE, SIDE, WPAD, C), BF)] + scratch
    else:
        scratch = [pltpu.VMEM((WIN, WIN, WPAD, C), BF)] + scratch
    operands = [in_hbm(grid), *slabs, *weights]
    return call(
        forward_rest if slabs else forward_first,
        "window_forward_rest" if slabs else "window_forward_first",
        count,
        [edges] + operands,
        [pl.BlockSpec(memory_space=pltpu.SMEM)] + whole_specs(operands),
        out + saved,
        scratch,
        5.0 * count,
    )


def backward_call(kernel, name, grid, slabs, saved, skip, tables, extra, count, outs, scratch, core=None):
    lead = [in_hbm(grid), *slabs]
    specs = whole_specs(lead)
    specs += [per_pair((2,) + shape, skip) for shape, _ in SAVED]
    specs += whole_specs([*tables, *extra])
    side = SIDE if slabs else WIN
    scratch = [
        pltpu.VMEM((side, side, WPAD, C), BF),
        pltpu.VMEM((2, C, LROWS), F32),
        *scratch,
    ]
    outs = [(per_pair(PAIR), pltpu.HBM((count,) + PAIR[1:], BF))] + [
        (whole(o.shape), o) for o in outs
    ]
    operands = [*lead, *[in_hbm(s) for s in saved], *tables, *extra]
    if core is not None:
        operands.append(core)
        specs.append(pl.BlockSpec(memory_space=pltpu.SMEM))
    return call(kernel, name, count, operands, specs, outs, scratch, 12.0 * count)


def place_trailing(target, first, rest, behind_d, behind_h, behind_dh):
    split = KEEP - WIN
    target[SHIFT : SHIFT + WIN, SHIFT : SHIFT + WIN, 0:SIDE, :] = first[0]
    target[SHIFT : SHIFT + WIN, SHIFT + WIN :, 0:SIDE, :] = rest[0][:, :split]
    target[SHIFT + WIN :, SHIFT : SHIFT + WIN, 0:SIDE, :] = rest[1][:split]
    target[SHIFT + WIN :, SHIFT + WIN :, 0:SIDE, :] = rest[2][:split, :split]
    target[0:SHIFT, SHIFT:, 0:SIDE, :] = behind_d[...]
    target[SHIFT:, 0:SHIFT, 0:SIDE, :] = behind_h[...]
    target[0:SHIFT, 0:SHIFT, 0:SIDE, :] = behind_dh[...]


def merge_kernel(
    tokens,
    first,
    rest,
    behind_d,
    behind_h,
    behind_dh,
    cotangent,
    weight,
    gather,
    scatter,
    high_out,
    low_out,
    main_out,
    slab_d,
    slab_h,
    slab_dh,
    block,
    pieces,
):
    block[:, :, SIDE:, :] = jnp.zeros((SIDE, SIDE, WPAD - SIDE, C), BF)
    place_trailing(block, first, rest, behind_d, behind_h, behind_dh)
    block[:, :, 0:SIDE, :] = (
        tokens[...].astype(F32) + block[:, :, 0:SIDE, :].astype(F32)
    ).astype(BF)
    total = jnp.zeros((ROWS, 1), F32)
    for pair in range(4):
        a, b = pair // 2, pair % 2
        part = block[...].reshape(WIN, 2, WIN, 2, WPAD, C)[:, a, :, b]
        both = gather_groups(gather, part.reshape(GROUP, C))
        for c in range(2):
            piece = both[c]
            pieces[2 * pair + c] = piece
            total = total + jnp.sum(piece, axis=-1, keepdims=True)
    mean = total / (8 * C)
    square = jnp.zeros((ROWS, 1), F32)
    for index in range(8):
        centre = pieces[index] - mean
        square = square + jnp.sum(centre * centre, axis=-1, keepdims=True)
    inv_std = lax.rsqrt(square / (8 * C) + EPSILON)
    grad_sum = jnp.zeros((ROWS, 1), F32)
    cross_sum = jnp.zeros((ROWS, 1), F32)
    cot = cotangent[...]
    for index in range(8):
        normed = (pieces[index] - mean) * inv_std
        part = dot_tn(normed.astype(BF), cot).astype(BF)
        for tile in range(3):
            start = (tile * 8 + index) * C
            main_out[start : start + C, :] = part[:, tile * TILE : (tile + 1) * TILE]
        grad = dot_nt(cot, weight[index])
        grad_sum = grad_sum + jnp.sum(grad, axis=-1, keepdims=True)
        cross_sum = cross_sum + jnp.sum(grad * normed, axis=-1, keepdims=True)
    grad_mean = grad_sum / (8 * C)
    cross_mean = cross_sum / (8 * C)
    for a in range(2):
        highs, lows = [], []
        for b in range(2):
            high_pair, low_pair = [], []
            for c in range(2):
                index = 4 * a + 2 * b + c
                normed = (pieces[index] - mean) * inv_std
                grad = dot_nt(cot, weight[index])
                grad = inv_std * (grad - grad_mean - normed * cross_mean)
                high = grad.astype(BF)
                high_pair.append(high)
                low_pair.append((grad - high.astype(F32)).astype(BF))
            for pair, kept in ((high_pair, highs), (low_pair, lows)):
                laid = scatter_groups(scatter, pair).astype(BF)
                kept.append(laid.reshape(WIN, WIN, WPAD, C))
        for kept, out in ((highs, high_out), (lows, low_out)):
            merged = jnp.stack(kept, axis=2).reshape(WIN, SIDE, WPAD, C)
            for i in range(WIN):
                out[2 * i + a] = merged[i, :, :SIDE, :]
    slab_d[...] = high_out[:SHIFT, SHIFT:]
    slab_h[...] = high_out[SHIFT:, :SHIFT]
    slab_dh[...] = high_out[:SHIFT, :SHIFT]


def final_kernel(
    tokens, high, low, first, rest, behind_d, behind_h, behind_dh, _, out, grads
):
    place_trailing(grads, first, rest, behind_d, behind_h, behind_dh)

    @pl.loop(0, SIDE)
    def row(d):
        normed, inv_std = norm_rows(tokens[d].astype(F32))
        grad = grads[d].astype(F32)
        back = inv_std * (
            grad
            - jnp.mean(grad, axis=-1, keepdims=True)
            - normed * jnp.mean(grad * normed, axis=-1, keepdims=True)
        )
        out[d] = (high[d].astype(F32) + low[d].astype(F32) + back).astype(BF)


def merge_call(tokens, first, rest, slabs, cot_rows, weight, parity):
    operands = [in_hbm(tokens), in_hbm(first), in_hbm(rest), *slabs, cot_rows, in_hbm(weight), *parity]
    shapes = [GRID, GRID, (MAIN, TILE), *SLABS]
    kinds = [pltpu.HBM, pltpu.HBM, pltpu.HBM, struct, struct, struct]
    return call(
        merge_kernel,
        "merge_backward",
        1,
        operands,
        whole_specs(operands),
        [(whole(s), kind(s, BF)) for s, kind in zip(shapes, kinds)],
        [pltpu.VMEM((SIDE, SIDE, WPAD, C), BF), pltpu.VMEM((8, ROWS, C), F32)],
        10.0,
    )


def final_call(tokens, high, low, first, rest, slabs, after):
    operands = [in_hbm(a) for a in (tokens, high, low, first, rest)] + [*slabs]
    return call(
        final_kernel,
        "token_gradient",
        1,
        operands + [after],
        whole_specs(operands) + [pl.BlockSpec(memory_space=pl.ANY)],
        [(whole(GRID), struct(GRID, BF))],
        [pltpu.VMEM(GRID, BF)],
        7.0,
    )[0]


def moved(value, steps_d, steps_h):
    count_d, count_h = lax.axis_size("gx"), lax.axis_size("gy")
    pairs = []
    for d in range(count_d):
        for h in range(count_h):
            target = (d + steps_d) % count_d * count_h + (h + steps_h) % count_h
            pairs.append((d * count_h + h, target))
    return lax.ppermute(value, ("gx", "gy"), pairs)


def sent_back(slabs):
    d, h, dh = slabs
    return moved(d, -1, 0), moved(h, 0, -1), moved(dh, -1, -1)


def sent_on(slabs):
    d, h, dh = slabs
    return moved(d, 1, 0), moved(h, 0, 1), moved(dh, 1, 1)


def same_core():
    count_d, count_h = lax.axis_size("gx"), lax.axis_size("gy")
    return [
        [d * count_h + h for d in range(core, count_d, 2) for h in range(count_h)]
        for core in range(2)
    ]


def exchanged(blocks):
    return lax.all_to_all(
        blocks, ("gx", "gy"), 0, 0, axis_index_groups=same_core(), tiled=True
    )


def swapped(value):
    count_d, count_h = lax.axis_size("gx"), lax.axis_size("gy")
    pairs = [
        (d * count_h + h, (d ^ 1) * count_h + h) for d in range(count_d) for h in range(count_h)
    ]
    return lax.ppermute(value, ("gx", "gy"), pairs)


def block_sum(half):
    count = len(same_core()[0])
    blocks = exchanged(half.reshape(count, half.shape[0] // count, TILE))
    return jnp.sum(blocks.astype(F32), axis=0).astype(BF)


def block_spread(own):
    count = len(same_core()[0])
    spread = exchanged(jnp.broadcast_to(own[None], (count,) + own.shape))
    return spread.reshape(count * own.shape[0], TILE)


def local(tokens, qkv_weight, proj_weight, merge_weight, cotangent):
    gather = jnp.asarray(window_table(), BF)
    scatter = jnp.asarray(window_table().T, BF)
    parity = (jnp.asarray(parity_table(), BF), jnp.asarray(parity_table().T, BF))
    codes = jnp.asarray(class_codes())
    masks = jnp.asarray(head_masks(), BF)
    spread = jnp.asarray(head_spread()[:C], BF)
    edges = jnp.stack(
        [
            (lax.axis_index("gx") == lax.axis_size("gx") - 1).astype(jnp.int32),
            (lax.axis_index("gy") == lax.axis_size("gy") - 1).astype(jnp.int32),
        ]
    )
    split = qkv_weight.reshape(C, 3, C).transpose(1, 0, 2)
    scaled = jnp.concatenate([split[:1] * BF(HD**-0.5), split[1:]], axis=0)
    scaled = jnp.pad(scaled, ((0, 0), (0, 0), (0, WIDE - C)))
    turned = split[1:].transpose(0, 2, 1)
    wproj_wide = jnp.pad(proj_weight, ((0, WIDE - C), (0, 0)))
    cot_rows = jnp.pad(cotangent.reshape(TOK, 2 * C), ((0, ROWS - TOK), (0, 0)))
    weight = merge_weight.reshape(8, C, 2 * C)

    ahead = sent_back(
        (tokens[:SHIFT, SHIFT:], tokens[SHIFT:, :SHIFT], tokens[:SHIFT, :SHIFT])
    )
    weights = (scaled, turned, proj_weight, gather, scatter, codes, masks)
    first, *saved_first = forward_call(edges, tokens, (), weights, 1)
    rest, slab_d, slab_h, slab_dh, *saved_rest = forward_call(
        edges, tokens, ahead, weights, 3
    )
    high, low, main, *slabs = merge_call(
        tokens,
        first,
        rest,
        sent_on((slab_d, slab_h, slab_dh)),
        cot_rows,
        weight,
        parity,
    )
    ahead = sent_back(slabs)
    tables = (qkv_weight, wproj_wide, gather, scatter, masks, spread)
    sums = [struct((C, 3 * C), F32), struct((C, C), F32)]
    first, qkv_sum, proj_sum = backward_call(
        backward_first, "window_backward_first", high, (), saved_first, 0, tables, (), 1, sums, ()
    )
    core = lax.rem(lax.axis_index("gx"), 2).astype(jnp.int32).reshape(1)
    rest, kept, given = backward_call(
        backward_rest,
        "window_backward_rest",
        high,
        ahead,
        saved_rest,
        0,
        tables,
        (qkv_sum, proj_sum, in_hbm(main)),
        3,
        [struct((HALF, TILE), BF), struct((HALF, TILE), BF)],
        [
            pltpu.VMEM((C, 3 * C), F32),
            pltpu.VMEM((C, C), F32),
            pltpu.VMEM((LATE, TILE), BF),
        ],
        core,
    )
    half = (kept.astype(F32) + swapped(given).astype(F32)).astype(BF)
    at = KEEP - WIN
    slabs = (
        jnp.concatenate([rest[1][at:], rest[2][at:, :at]], axis=1),
        jnp.concatenate([rest[0][:, at:], rest[2][:at, at:]], axis=0),
        rest[2][at:, at:],
    )
    behind = sent_on(slabs)
    late, *behind = lax.optimization_barrier((block_sum(half), *behind))
    token_grad = final_call(tokens, high, low, first, rest, behind, late)
    late = block_spread(late)
    shapes = [(C, 3 * C), (C, C), (8 * C, 2 * C)]
    weight_grads = call(
        unpack_kernel,
        "unpack",
        1,
        [core, late, swapped(late)],
        [pl.BlockSpec(memory_space=pltpu.SMEM)] + whole_specs([late, late]),
        [(whole(s), struct(s, F32)) for s in shapes],
        [],
        1.0,
    )
    return (token_grad, *weight_grads)


def solution(mesh):
    placed = (P("gx", "gy", None, None), P(), P(), P(), P("gx", "gy", None, None))
    return jax.shard_map(
        local,
        mesh=mesh,
        in_specs=placed,
        out_specs=(P("gx", "gy", None, None), P(), P(), P()),
        check_vma=False,
    )
```

```python
import jax
import jax.numpy as jnp
import numpy as np
from jax import lax
from jax.experimental import pallas as pl
from jax.experimental.pallas import tpu as pltpu
from jax.sharding import PartitionSpec as P

C = 192
HEADS = 12
HD = 16
WIN = 7
SHIFT = 3
SIDE = 14
WPAD = 16
TOK = WIN**3
ROWS = 352
LROWS = 384
WIDE = 256
GROUP = WIN * WIN * WPAD
TILE = 128
CHUNK = 16
SPAN = CHUNK * WIN
FULL = WIN * WIN // CHUNK
TILES = 6
MAIN = 4608
LATE = 6144
HALF = LATE // 2
STAT = 192
LABEL = 228
CLASSES = 8
FAR = 1e30
EPSILON = 1e-05
BF = jnp.bfloat16
F32 = jnp.float32
VMEM_LIMIT = 40 * 2**20


def head_masks():
    mask = np.zeros((HEADS, WIDE), np.float32)
    for head in range(HEADS):
        mask[head, head * HD : (head + 1) * HD] = 1
        for part in range(3):
            mask[head, STAT + part * HEADS + head] = 1
        mask[head, LABEL : LABEL + CLASSES] = 1
    return mask


def head_spread():
    spread = np.zeros((WIDE, WIDE), np.float32)
    for head in range(HEADS):
        for part in range(3):
            spread[head * HD : (head + 1) * HD, STAT + part * HEADS + head] = 1
    return spread


def group_table(width_of):
    table = np.zeros((2, CHUNK * WIN, CHUNK * WPAD), np.float32)
    for half in range(2):
        for pair in range(CHUNK):
            for place in range(WIN):
                table[half, pair * WIN + place, pair * WPAD + width_of(half, place)] = 1
    return table.reshape(2 * CHUNK * WIN, CHUNK * WPAD)


def window_table():
    return group_table(lambda half, place: (half * WIN + place + SHIFT) % SIDE)


def parity_table():
    return group_table(lambda parity, place: 2 * place + parity)


def class_codes():
    codes = np.full((LROWS, 1), CLASSES, np.int32)
    for place in range(TOK):
        i, j, k = place // (WIN * WIN), place // WIN % WIN, place % WIN
        codes[place, 0] = 4 * (i >= 4) + 2 * (j >= 4) + (k >= 4)
    return codes


def dot(a, b):
    return lax.dot_general(a, b, (((1,), (0,)), ((), ())), preferred_element_type=F32)


def dot_nt(a, b):
    return lax.dot_general(a, b, (((1,), (1,)), ((), ())), preferred_element_type=F32)


def dot_tn(a, b):
    return lax.dot_general(a, b, (((0,), (0,)), ((), ())), preferred_element_type=F32)


def gather_groups(table, block):
    halves = ([], [])
    for chunk in range(FULL):
        start = chunk * CHUNK * WPAD
        both = dot(table[...], block[start : start + CHUNK * WPAD])
        for half in range(2):
            halves[half].append(both[half * SPAN : (half + 1) * SPAN])
    tail = jnp.concatenate([table[:WPAD, :TILE], table[SPAN : SPAN + WPAD, :TILE]], axis=0)
    end = block[FULL * CHUNK * WPAD :]
    end = jnp.concatenate([end, jnp.zeros((TILE - WPAD, end.shape[1]), end.dtype)], axis=0)
    both = dot(tail, end)
    for half in range(2):
        halves[half].append(both[half * WPAD : (half + 1) * WPAD])
    return [jnp.concatenate(rows, axis=0) for rows in halves]


def scatter_groups(table, halves):
    out = []
    for chunk in range(FULL):
        rows = slice(chunk * SPAN, (chunk + 1) * SPAN)
        out.append(dot(table[...], jnp.concatenate([h[rows] for h in halves], axis=0)))
    pad = jnp.zeros((SPAN - WPAD, halves[0].shape[1]), halves[0].dtype)
    tail = [part for h in halves for part in (h[FULL * SPAN :], pad)]
    out.append(dot(table[:WPAD, :], jnp.concatenate(tail, axis=0)))
    return jnp.concatenate(out, axis=0)


def three_parts(value):
    high = value.astype(BF)
    rest = value - high.astype(F32)
    middle = rest.astype(BF)
    low = (rest - middle.astype(F32)).astype(BF)
    return high, middle, low


def dot_exact(value, table):
    high, middle, low = three_parts(value)
    return dot(high, table) + dot(middle, table) + dot(low, table)


def stat_lanes(value, lane):
    high, middle, low = three_parts(value)
    mixed = jnp.where(
        lane < STAT + HEADS,
        high.astype(F32),
        jnp.where(lane < STAT + 2 * HEADS, middle.astype(F32), low.astype(F32)),
    )
    return jnp.where((lane >= STAT) & (lane < STAT + 3 * HEADS), mixed, 0.0)


def norm_rows(values):
    centre = values - jnp.mean(values, axis=-1, keepdims=True)
    inv_std = lax.rsqrt(jnp.mean(centre * centre, axis=-1, keepdims=True) + EPSILON)
    return (centre * inv_std, inv_std)


def place_rolled(rolled, own, ahead_d, ahead_h, ahead_dh):
    keep = SIDE - SHIFT
    rolled[:, :, SIDE:, :] = jnp.zeros((SIDE, SIDE, WPAD - SIDE, C), rolled.dtype)
    rolled[0:keep, 0:keep, 0:SIDE, :] = own[SHIFT:, SHIFT:, :, :]
    rolled[keep:, 0:keep, 0:SIDE, :] = ahead_d[...]
    rolled[0:keep, keep:, 0:SIDE, :] = ahead_h[...]
    rolled[keep:, keep:, 0:SIDE, :] = ahead_dh[...]


def pair_corner(pair):
    return WIN * lax.div(pair, 2), WIN * lax.rem(pair, 2)


def forward_pair(
    wd,
    wh,
    block,
    edges,
    wqkv,
    wturned,
    wproj,
    gather,
    scatter,
    codes,
    masks,
    rows_out,
    q_out,
    k_out,
    kt_out,
    v_out,
    mixed_out,
    mixed_t,
    stat_t,
):
    lane = lax.broadcasted_iota(jnp.int32, (1, WIDE), 1)
    in_labels = (lane >= LABEL) & (lane < LABEL + CLASSES)
    in_stats = (lane >= STAT) & (lane < STAT + 3 * HEADS)
    normed, _ = norm_rows(block.reshape(GROUP, C).astype(F32))
    pad = jnp.zeros((LROWS - ROWS, C), BF)
    both = gather_groups(gather, normed.astype(BF))
    halves = []
    for half in range(2):
        rows = jnp.concatenate([both[half].astype(BF), pad], axis=0)
        rows_out[half] = rows[:ROWS]
        q = dot(rows, wqkv[0])
        k = dot(rows, wqkv[1])
        v = dot(rows, wqkv[2])
        kt_out[half] = dot_nt(wturned[0], rows).astype(BF)[:, :ROWS]
        vt = dot_nt(wturned[1], rows).astype(BF)[:, :ROWS]
        allowed = (
            4 * jnp.where(wd == 1, edges[0], 0)
            + 2 * jnp.where(wh == 1, edges[1], 0)
            + half
            + CLASSES
        )
        here = lane == LABEL + (codes[...] & allowed)
        q_aug = jnp.where(in_labels, jnp.where(here, 1.0, 0.0), q).astype(BF)
        k_aug = jnp.where(
            in_labels, jnp.where(here, 0.0, -FAR), jnp.where(in_stats, -1.0, k)
        ).astype(BF)[:ROWS]
        v_aug = jnp.where(in_stats, -1.0, v).astype(BF)[:ROWS]
        stat_t[half] = jnp.zeros((WIDE - TILE, LROWS), F32)
        for two in range(HEADS // 2):
            q_m = jnp.concatenate(
                [q_aug * masks[h : h + 1, :] for h in (2 * two, 2 * two + 1)], axis=0
            )
            scores = dot_nt(k_aug, q_m)
            top = jnp.max(scores, axis=0, keepdims=True)
            expo = jnp.exp(scores - top)
            sums = jnp.sum(expo, axis=0, keepdims=True)
            probs = (expo * (1.0 / sums)).astype(BF)
            stats = top + jnp.log(sums)
            mixed = dot(vt[2 * HD * two : 2 * HD * (two + 1)], probs)
            for i in range(2):
                h = 2 * two + i
                lanes = slice(i * LROWS, (i + 1) * LROWS)
                mixed_t[half, h * HD : (h + 1) * HD, :] = mixed[i * HD : (i + 1) * HD, lanes]
                for part in range(3):
                    row = STAT - TILE + part * HEADS + h
                    stat_t[half, row : row + 1, :] = stats[:, lanes]
        mixed = mixed_t[half].T[:ROWS]
        mixed_out[half] = mixed
        q_out[half, :, :TILE] = q_aug[:, :TILE]
        stats = stat_lanes(stat_t[half].T, lane[:, TILE:])
        q_out[half, :, TILE:] = (q_aug[:, TILE:].astype(F32) + stats).astype(BF)
        k_out[half] = k_aug
        v_out[half] = v_aug
        halves.append(dot(mixed.astype(BF), wproj[...]).astype(BF))
    back = scatter_groups(scatter, halves).astype(BF)
    return back.reshape(WIN, WIN, WPAD, C)[:, :, :SIDE, :]


def first_block(block, own):
    block[:, :, SIDE:, :] = jnp.zeros((WIN, WIN, WPAD - SIDE, C), BF)
    block[:, :, 0:SIDE, :] = own[SHIFT : SHIFT + WIN, SHIFT : SHIFT + WIN, :, :]
    return block[...]


def forward_first(edges, own, *refs):
    *weights, out, rows, q, k, kt, v, mixed, block, mixed_t, stat_t = refs
    out[0] = forward_pair(
        0, 0, first_block(block, own), edges, *weights, rows, q, k, kt, v, mixed, mixed_t, stat_t
    )


def forward_rest(edges, own, ahead_d, ahead_h, ahead_dh, *refs):
    (
        *weights,
        out,
        slab_d,
        slab_h,
        slab_dh,
        rows,
        q,
        k,
        kt,
        v,
        mixed,
        rolled,
        mixed_t,
        stat_t,
    ) = refs
    pair = pl.program_id(0) + 1

    @pl.when(pair == 1)
    def _():
        place_rolled(rolled, own, ahead_d, ahead_h, ahead_dh)

    at_d, at_h = pair_corner(pair)
    block = rolled[pl.ds(at_d, WIN), pl.ds(at_h, WIN), :, :]
    out[0] = forward_pair(
        lax.div(pair, 2),
        lax.rem(pair, 2),
        block,
        edges,
        *weights,
        rows,
        q,
        k,
        kt,
        v,
        mixed,
        mixed_t,
        stat_t,
    )
    split = KEEP - WIN

    @pl.when(pair == 1)
    def _():
        slab_h[0:WIN] = out[0, :, split:]

    @pl.when(pair == 2)
    def _():
        slab_d[:, 0:WIN] = out[0, split:]

    @pl.when(pair == 3)
    def _():
        slab_h[WIN:] = out[0, :split, split:]
        slab_d[:, WIN:] = out[0, split:, :split]
        slab_dh[...] = out[0, split:, split:]


def backward_pair(
    block,
    rows_in,
    q_in,
    k_in,
    kt_in,
    v_in,
    mixed_in,
    wqkv,
    wproj,
    gather,
    scatter,
    masks,
    spread,
    qkv_sum,
    proj_sum,
    grad_t,
):
    lane = lax.broadcasted_iota(jnp.int32, (1, WIDE), 1)
    pad = jnp.zeros((LROWS - ROWS, C), BF)
    both = gather_groups(gather, block.reshape(GROUP, C))
    halves = []
    for half in range(2):
        grads = jnp.concatenate([both[half].astype(BF), pad], axis=0)
        mixed = mixed_in[half]
        proj_sum[...] += dot_tn(mixed.astype(BF), grads[:ROWS])
        grad_o = dot_nt(grads, wproj[...]).astype(BF)
        delta = dot_exact(mixed * grad_o[:ROWS, :C].astype(F32), spread[...])
        delta = jnp.concatenate(
            [stat_lanes(delta, lane), jnp.zeros((LROWS - ROWS, WIDE), F32)], axis=0
        )
        o_aug = (grad_o.astype(F32) + delta).astype(BF)
        q_aug = q_in[half]
        k_aug = k_in[half]
        v_aug = v_in[half]
        grad_k = jnp.zeros((ROWS, WIDE), F32)
        grad_v = jnp.zeros((ROWS, WIDE), F32)
        for two in range(HEADS // 2):
            heads = (2 * two, 2 * two + 1)
            q_m = jnp.concatenate([q_aug * masks[h : h + 1, :] for h in heads], axis=0)
            o_m = jnp.concatenate([o_aug * masks[h : h + 1, :] for h in heads], axis=0)
            probs = jnp.exp(dot_nt(k_aug, q_m))
            slopes = (probs * dot_nt(v_aug, o_m)).astype(BF)
            grad_v = grad_v + dot(probs.astype(BF), o_m)
            grad_k = grad_k + dot(slopes, q_m)
            turned = dot(kt_in[half, 2 * HD * two : 2 * HD * (two + 1), :], slopes)
            for i, h in enumerate(heads):
                grad_t[half, h * HD : (h + 1) * HD, :] = turned[
                    i * HD : (i + 1) * HD, i * LROWS : (i + 1) * LROWS
                ]
        grad_q = (grad_t[half].T[:ROWS] * HD**-0.5).astype(BF)
        grad = jnp.concatenate(
            [grad_q, grad_k[:, :C].astype(BF), grad_v[:, :C].astype(BF)], axis=1
        )
        qkv_sum[...] += dot_tn(rows_in[half], grad)
        halves.append(dot_nt(grad, wqkv[...]).astype(BF))
    back = scatter_groups(scatter, halves).astype(BF)
    return back.reshape(WIN, WIN, WPAD, C)[:, :, :SIDE, :]


def backward_first(own, *refs):
    *inputs, out, qkv_sum, proj_sum, block, grad_t = refs
    qkv_sum[...] = jnp.zeros_like(qkv_sum)
    proj_sum[...] = jnp.zeros_like(proj_sum)
    out[0] = backward_pair(first_block(block, own), *inputs, qkv_sum, proj_sum, grad_t)


def backward_rest(own, ahead_d, ahead_h, ahead_dh, *refs):
    (
        *inputs,
        qkv_in,
        proj_in,
        main,
        core,
        out,
        kept,
        given,
        rolled,
        grad_t,
        qkv_sum,
        proj_sum,
        late,
    ) = refs
    pair = pl.program_id(0) + 1

    @pl.when(pair == 1)
    def _():
        place_rolled(rolled, own, ahead_d, ahead_h, ahead_dh)
        qkv_sum[...] = qkv_in[...]
        proj_sum[...] = proj_in[...]
        late[0:MAIN, :] = main[...]
        late[MAIN + TILES * C :, :] = jnp.zeros((LATE - MAIN - TILES * C, TILE), BF)

    at_d, at_h = pair_corner(pair)
    block = rolled[pl.ds(at_d, WIN), pl.ds(at_h, WIN), :, :]
    out[0] = backward_pair(block, *inputs, qkv_sum, proj_sum, grad_t)

    @pl.when(pair == 3)
    def _():
        table = jnp.concatenate([qkv_sum[...], proj_sum[...]], axis=1).astype(BF)
        for tile in range(TILES):
            start = MAIN + tile * C
            late[start : start + C, :] = table[:, tile * TILE : (tile + 1) * TILE]
        kept[...] = late[pl.ds(core[0] * HALF, HALF), :]
        given[...] = late[pl.ds((1 - core[0]) * HALF, HALF), :]


def unpack_kernel(core, mine, other, qkv_out, proj_out, merge_out):
    first = core[0] == 0
    low = jnp.where(first, mine[...].astype(F32), other[...].astype(F32))
    high = jnp.where(first, other[...].astype(F32), mine[...].astype(F32))
    rows = 8 * C
    for tile, part in enumerate((low[:rows], low[rows:], high[:rows])):
        merge_out[:, tile * TILE : (tile + 1) * TILE] = part
    rest = high[rows:]
    table = jnp.concatenate(
        [rest[tile * C : (tile + 1) * C, :] for tile in range(TILES)], axis=1
    )
    qkv_out[...] = table[:, : 3 * C]
    proj_out[...] = table[:, 3 * C :]


def whole(shape):
    return pl.BlockSpec(shape, lambda step: (0,) * len(shape))


def per_pair(shape, first=0):
    return pl.BlockSpec(shape, lambda step: (step + first,) + (0,) * (len(shape) - 1))


KEEP = SIDE - SHIFT
GRID = (SIDE, SIDE, SIDE, C)
SLABS = ((SHIFT, KEEP, SIDE, C), (KEEP, SHIFT, SIDE, C), (SHIFT, SHIFT, SIDE, C))
SAVED = (
    ((ROWS, C), BF),
    ((LROWS, WIDE), BF),
    ((ROWS, WIDE), BF),
    ((C, ROWS), BF),
    ((ROWS, WIDE), BF),
    ((ROWS, C), F32),
)
PAIR = (1, WIN, WIN, SIDE, C)


def struct(shape, dtype):
    return jax.ShapeDtypeStruct(shape, dtype)


def call(kernel, name, count, operands, in_specs, outs, scratch, gigaflops):
    return pl.pallas_call(
        kernel,
        grid=(count,),
        in_specs=in_specs,
        out_specs=[spec for spec, _ in outs],
        out_shape=[shape for _, shape in outs],
        scratch_shapes=scratch,
        compiler_params=pltpu.CompilerParams(
            dimension_semantics=("arbitrary",), vmem_limit_bytes=VMEM_LIMIT
        ),
        cost_estimate=pl.CostEstimate(
            flops=int(gigaflops * 1e9), bytes_accessed=8 * 2**20, transcendentals=0
        ),
        name=name,
    )(*operands)


def in_hbm(array):
    return pltpu.with_memory_space_constraint(array, pltpu.HBM)


def whole_specs(arrays):
    return [whole(a.shape) for a in arrays]


def forward_call(edges, grid, slabs, weights, count):
    saved = [
        (per_pair((2,) + shape), pltpu.HBM((2 * count,) + shape, dtype))
        for shape, dtype in SAVED
    ]
    out = [(per_pair(PAIR), pltpu.HBM((count,) + PAIR[1:], BF))]
    scratch = [pltpu.VMEM((2, C, LROWS), F32), pltpu.VMEM((2, WIDE - TILE, LROWS), F32)]
    if slabs:
        out += [(whole(s), struct(s, BF)) for s in SLABS]
        scratch = [pltpu.VMEM((SIDE, SIDE, WPAD, C), BF)] + scratch
    else:
        scratch = [pltpu.VMEM((WIN, WIN, WPAD, C), BF)] + scratch
    operands = [in_hbm(grid), *slabs, *weights]
    return call(
        forward_rest if slabs else forward_first,
        "window_forward_rest" if slabs else "window_forward_first",
        count,
        [edges] + operands,
        [pl.BlockSpec(memory_space=pltpu.SMEM)] + whole_specs(operands),
        out + saved,
        scratch,
        5.0 * count,
    )


def backward_call(kernel, name, grid, slabs, saved, skip, tables, extra, count, outs, scratch, core=None):
    lead = [in_hbm(grid), *slabs]
    specs = whole_specs(lead)
    specs += [per_pair((2,) + shape, skip) for shape, _ in SAVED]
    specs += whole_specs([*tables, *extra])
    side = SIDE if slabs else WIN
    scratch = [
        pltpu.VMEM((side, side, WPAD, C), BF),
        pltpu.VMEM((2, C, LROWS), F32),
        *scratch,
    ]
    outs = [(per_pair(PAIR), pltpu.HBM((count,) + PAIR[1:], BF))] + [
        (whole(o.shape), o) for o in outs
    ]
    operands = [*lead, *[in_hbm(s) for s in saved], *tables, *extra]
    if core is not None:
        operands.append(core)
        specs.append(pl.BlockSpec(memory_space=pltpu.SMEM))
    return call(kernel, name, count, operands, specs, outs, scratch, 12.0 * count)


def place_trailing(target, first, rest, behind_d, behind_h, behind_dh):
    split = KEEP - WIN
    target[SHIFT : SHIFT + WIN, SHIFT : SHIFT + WIN, 0:SIDE, :] = first[0]
    target[SHIFT : SHIFT + WIN, SHIFT + WIN :, 0:SIDE, :] = rest[0][:, :split]
    target[SHIFT + WIN :, SHIFT : SHIFT + WIN, 0:SIDE, :] = rest[1][:split]
    target[SHIFT + WIN :, SHIFT + WIN :, 0:SIDE, :] = rest[2][:split, :split]
    target[0:SHIFT, SHIFT:, 0:SIDE, :] = behind_d[...]
    target[SHIFT:, 0:SHIFT, 0:SIDE, :] = behind_h[...]
    target[0:SHIFT, 0:SHIFT, 0:SIDE, :] = behind_dh[...]


def merge_kernel(
    tokens,
    first,
    rest,
    behind_d,
    behind_h,
    behind_dh,
    cotangent,
    weight,
    gather,
    scatter,
    high_out,
    low_out,
    main_out,
    slab_d,
    slab_h,
    slab_dh,
    block,
    pieces,
):
    block[:, :, SIDE:, :] = jnp.zeros((SIDE, SIDE, WPAD - SIDE, C), BF)
    place_trailing(block, first, rest, behind_d, behind_h, behind_dh)
    block[:, :, 0:SIDE, :] = (
        tokens[...].astype(F32) + block[:, :, 0:SIDE, :].astype(F32)
    ).astype(BF)
    total = jnp.zeros((ROWS, 1), F32)
    for pair in range(4):
        a, b = pair // 2, pair % 2
        part = block[...].reshape(WIN, 2, WIN, 2, WPAD, C)[:, a, :, b]
        both = gather_groups(gather, part.reshape(GROUP, C))
        for c in range(2):
            piece = both[c]
            pieces[2 * pair + c] = piece
            total = total + jnp.sum(piece, axis=-1, keepdims=True)
    mean = total / (8 * C)
    square = jnp.zeros((ROWS, 1), F32)
    for index in range(8):
        centre = pieces[index] - mean
        square = square + jnp.sum(centre * centre, axis=-1, keepdims=True)
    inv_std = lax.rsqrt(square / (8 * C) + EPSILON)
    grad_sum = jnp.zeros((ROWS, 1), F32)
    cross_sum = jnp.zeros((ROWS, 1), F32)
    cot = cotangent[...]
    for index in range(8):
        normed = (pieces[index] - mean) * inv_std
        part = dot_tn(normed.astype(BF), cot).astype(BF)
        for tile in range(3):
            start = (tile * 8 + index) * C
            main_out[start : start + C, :] = part[:, tile * TILE : (tile + 1) * TILE]
        grad = dot_nt(cot, weight[index])
        grad_sum = grad_sum + jnp.sum(grad, axis=-1, keepdims=True)
        cross_sum = cross_sum + jnp.sum(grad * normed, axis=-1, keepdims=True)
    grad_mean = grad_sum / (8 * C)
    cross_mean = cross_sum / (8 * C)
    for a in range(2):
        highs, lows = [], []
        for b in range(2):
            high_pair, low_pair = [], []
            for c in range(2):
                index = 4 * a + 2 * b + c
                normed = (pieces[index] - mean) * inv_std
                grad = dot_nt(cot, weight[index])
                grad = inv_std * (grad - grad_mean - normed * cross_mean)
                high = grad.astype(BF)
                high_pair.append(high)
                low_pair.append((grad - high.astype(F32)).astype(BF))
            for pair, kept in ((high_pair, highs), (low_pair, lows)):
                laid = scatter_groups(scatter, pair).astype(BF)
                kept.append(laid.reshape(WIN, WIN, WPAD, C))
        for kept, out in ((highs, high_out), (lows, low_out)):
            merged = jnp.stack(kept, axis=2).reshape(WIN, SIDE, WPAD, C)
            for i in range(WIN):
                out[2 * i + a] = merged[i, :, :SIDE, :]
    slab_d[...] = high_out[:SHIFT, SHIFT:]
    slab_h[...] = high_out[SHIFT:, :SHIFT]
    slab_dh[...] = high_out[:SHIFT, :SHIFT]


def final_kernel(
    tokens, high, low, first, rest, behind_d, behind_h, behind_dh, _, out, grads
):
    place_trailing(grads, first, rest, behind_d, behind_h, behind_dh)

    @pl.loop(0, SIDE)
    def row(d):
        normed, inv_std = norm_rows(tokens[d].astype(F32))
        grad = grads[d].astype(F32)
        back = inv_std * (
            grad
            - jnp.mean(grad, axis=-1, keepdims=True)
            - normed * jnp.mean(grad * normed, axis=-1, keepdims=True)
        )
        out[d] = (high[d].astype(F32) + low[d].astype(F32) + back).astype(BF)


def merge_call(tokens, first, rest, slabs, cot_rows, weight, parity):
    operands = [in_hbm(tokens), in_hbm(first), in_hbm(rest), *slabs, cot_rows, in_hbm(weight), *parity]
    shapes = [GRID, GRID, (MAIN, TILE), *SLABS]
    kinds = [pltpu.HBM, pltpu.HBM, pltpu.HBM, struct, struct, struct]
    return call(
        merge_kernel,
        "merge_backward",
        1,
        operands,
        whole_specs(operands),
        [(whole(s), kind(s, BF)) for s, kind in zip(shapes, kinds)],
        [pltpu.VMEM((SIDE, SIDE, WPAD, C), BF), pltpu.VMEM((8, ROWS, C), F32)],
        10.0,
    )


def final_call(tokens, high, low, first, rest, slabs, after):
    operands = [in_hbm(a) for a in (tokens, high, low, first, rest)] + [*slabs]
    return call(
        final_kernel,
        "token_gradient",
        1,
        operands + [after],
        whole_specs(operands) + [pl.BlockSpec(memory_space=pl.ANY)],
        [(whole(GRID), struct(GRID, BF))],
        [pltpu.VMEM(GRID, BF)],
        7.0,
    )[0]


def moved(value, steps_d, steps_h):
    count_d, count_h = lax.axis_size("gx"), lax.axis_size("gy")
    pairs = []
    for d in range(count_d):
        for h in range(count_h):
            target = (d + steps_d) % count_d * count_h + (h + steps_h) % count_h
            pairs.append((d * count_h + h, target))
    return lax.ppermute(value, ("gx", "gy"), pairs)


def sent_back(slabs):
    d, h, dh = slabs
    return moved(d, -1, 0), moved(h, 0, -1), moved(dh, -1, -1)


def sent_on(slabs):
    d, h, dh = slabs
    return moved(d, 1, 0), moved(h, 0, 1), moved(dh, 1, 1)


def same_core():
    count_d, count_h = lax.axis_size("gx"), lax.axis_size("gy")
    return [
        [d * count_h + h for d in range(core, count_d, 2) for h in range(count_h)]
        for core in range(2)
    ]


def exchanged(blocks):
    return lax.all_to_all(
        blocks, ("gx", "gy"), 0, 0, axis_index_groups=same_core(), tiled=True
    )


def swapped(value):
    count_d, count_h = lax.axis_size("gx"), lax.axis_size("gy")
    pairs = [
        (d * count_h + h, (d ^ 1) * count_h + h) for d in range(count_d) for h in range(count_h)
    ]
    return lax.ppermute(value, ("gx", "gy"), pairs)


def block_sum(half):
    count = len(same_core()[0])
    blocks = exchanged(half.reshape(count, half.shape[0] // count, TILE))
    return jnp.sum(blocks.astype(F32), axis=0).astype(BF)


def block_spread(own):
    count = len(same_core()[0])
    spread = exchanged(jnp.broadcast_to(own[None], (count,) + own.shape))
    return spread.reshape(count * own.shape[0], TILE)


def local(tokens, qkv_weight, proj_weight, merge_weight, cotangent):
    gather = jnp.asarray(window_table(), BF)
    scatter = jnp.asarray(window_table().T, BF)
    parity = (jnp.asarray(parity_table(), BF), jnp.asarray(parity_table().T, BF))
    codes = jnp.asarray(class_codes())
    masks = jnp.asarray(head_masks(), BF)
    spread = jnp.asarray(head_spread()[:C], BF)
    edges = jnp.stack(
        [
            (lax.axis_index("gx") == lax.axis_size("gx") - 1).astype(jnp.int32),
            (lax.axis_index("gy") == lax.axis_size("gy") - 1).astype(jnp.int32),
        ]
    )
    split = qkv_weight.reshape(C, 3, C).transpose(1, 0, 2)
    scaled = jnp.concatenate([split[:1] * BF(HD**-0.5), split[1:]], axis=0)
    scaled = jnp.pad(scaled, ((0, 0), (0, 0), (0, WIDE - C)))
    turned = split[1:].transpose(0, 2, 1)
    wproj_wide = jnp.pad(proj_weight, ((0, WIDE - C), (0, 0)))
    cot_rows = jnp.pad(cotangent.reshape(TOK, 2 * C), ((0, ROWS - TOK), (0, 0)))
    weight = merge_weight.reshape(8, C, 2 * C)

    ahead = sent_back(
        (tokens[:SHIFT, SHIFT:], tokens[SHIFT:, :SHIFT], tokens[:SHIFT, :SHIFT])
    )
    weights = (scaled, turned, proj_weight, gather, scatter, codes, masks)
    first, *saved_first = forward_call(edges, tokens, (), weights, 1)
    rest, slab_d, slab_h, slab_dh, *saved_rest = forward_call(
        edges, tokens, ahead, weights, 3
    )
    high, low, main, *slabs = merge_call(
        tokens,
        first,
        rest,
        sent_on((slab_d, slab_h, slab_dh)),
        cot_rows,
        weight,
        parity,
    )
    ahead = sent_back(slabs)
    tables = (qkv_weight, wproj_wide, gather, scatter, masks, spread)
    sums = [struct((C, 3 * C), F32), struct((C, C), F32)]
    first, qkv_sum, proj_sum = backward_call(
        backward_first, "window_backward_first", high, (), saved_first, 0, tables, (), 1, sums, ()
    )
    core = lax.rem(lax.axis_index("gx"), 2).astype(jnp.int32).reshape(1)
    rest, kept, given = backward_call(
        backward_rest,
        "window_backward_rest",
        high,
        ahead,
        saved_rest,
        0,
        tables,
        (qkv_sum, proj_sum, in_hbm(main)),
        3,
        [struct((HALF, TILE), BF), struct((HALF, TILE), BF)],
        [
            pltpu.VMEM((C, 3 * C), F32),
            pltpu.VMEM((C, C), F32),
            pltpu.VMEM((LATE, TILE), BF),
        ],
        core,
    )
    half = (kept.astype(F32) + swapped(given).astype(F32)).astype(BF)
    at = KEEP - WIN
    slabs = (
        jnp.concatenate([rest[1][at:], rest[2][at:, :at]], axis=1),
        jnp.concatenate([rest[0][:, at:], rest[2][:at, at:]], axis=0),
        rest[2][at:, at:],
    )
    behind = sent_on(slabs)
    late, *behind = lax.optimization_barrier((block_sum(half), *behind))
    token_grad = final_call(tokens, high, low, first, rest, behind, late)
    late, token_grad = lax.optimization_barrier((block_spread(late), token_grad))
    shapes = [(C, 3 * C), (C, C), (8 * C, 2 * C)]
    weight_grads = call(
        unpack_kernel,
        "unpack",
        1,
        [core, late, swapped(late)],
        [pl.BlockSpec(memory_space=pltpu.SMEM)] + whole_specs([late, late]),
        [(whole(s), struct(s, F32)) for s in shapes],
        [],
        1.0,
    )
    return (token_grad, *weight_grads)


def solution(mesh):
    placed = (P("gx", "gy", None, None), P(), P(), P(), P("gx", "gy", None, None))
    return jax.shard_map(
        local,
        mesh=mesh,
        in_specs=placed,
        out_specs=(P("gx", "gy", None, None), P(), P(), P()),
        check_vma=False,
    )
```

```python
import jax
import jax.numpy as jnp
import numpy as np
from jax import lax
from jax.experimental import pallas as pl
from jax.experimental.pallas import tpu as pltpu
from jax.sharding import PartitionSpec as P

C = 192
HEADS = 12
HD = 16
WIN = 7
SHIFT = 3
SIDE = 14
WPAD = 16
TOK = WIN**3
ROWS = 352
LROWS = 384
WIDE = 256
GROUP = WIN * WIN * WPAD
TILE = 128
CHUNK = 16
SPAN = CHUNK * WIN
FULL = WIN * WIN // CHUNK
TILES = 6
MAIN = 4608
LATE = 6144
HALF = LATE // 2
STAT = 192
LABEL = 228
CLASSES = 8
FAR = 1e30
EPSILON = 1e-05
BF = jnp.bfloat16
F32 = jnp.float32
VMEM_LIMIT = 40 * 2**20


def head_masks():
    mask = np.zeros((HEADS, WIDE), np.float32)
    for head in range(HEADS):
        mask[head, head * HD : (head + 1) * HD] = 1
        for part in range(3):
            mask[head, STAT + part * HEADS + head] = 1
        mask[head, LABEL : LABEL + CLASSES] = 1
    return mask


def head_spread():
    spread = np.zeros((WIDE, WIDE), np.float32)
    for head in range(HEADS):
        for part in range(3):
            spread[head * HD : (head + 1) * HD, STAT + part * HEADS + head] = 1
    return spread


def group_table(width_of):
    table = np.zeros((2, CHUNK * WIN, CHUNK * WPAD), np.float32)
    for half in range(2):
        for pair in range(CHUNK):
            for place in range(WIN):
                table[half, pair * WIN + place, pair * WPAD + width_of(half, place)] = 1
    return table.reshape(2 * CHUNK * WIN, CHUNK * WPAD)


def window_table():
    return group_table(lambda half, place: (half * WIN + place + SHIFT) % SIDE)


def parity_table():
    return group_table(lambda parity, place: 2 * place + parity)


def class_codes():
    codes = np.full((LROWS, 1), CLASSES, np.int32)
    for place in range(TOK):
        i, j, k = place // (WIN * WIN), place // WIN % WIN, place % WIN
        codes[place, 0] = 4 * (i >= 4) + 2 * (j >= 4) + (k >= 4)
    return codes


def dot(a, b):
    return lax.dot_general(a, b, (((1,), (0,)), ((), ())), preferred_element_type=F32)


def dot_nt(a, b):
    return lax.dot_general(a, b, (((1,), (1,)), ((), ())), preferred_element_type=F32)


def dot_tn(a, b):
    return lax.dot_general(a, b, (((0,), (0,)), ((), ())), preferred_element_type=F32)


def gather_groups(table, block):
    halves = ([], [])
    for chunk in range(FULL):
        start = chunk * CHUNK * WPAD
        both = dot(table[...], block[start : start + CHUNK * WPAD])
        for half in range(2):
            halves[half].append(both[half * SPAN : (half + 1) * SPAN])
    tail = jnp.concatenate([table[:WPAD, :TILE], table[SPAN : SPAN + WPAD, :TILE]], axis=0)
    end = block[FULL * CHUNK * WPAD :]
    end = jnp.concatenate([end, jnp.zeros((TILE - WPAD, end.shape[1]), end.dtype)], axis=0)
    both = dot(tail, end)
    for half in range(2):
        halves[half].append(both[half * WPAD : (half + 1) * WPAD])
    return [jnp.concatenate(rows, axis=0) for rows in halves]


def scatter_groups(table, halves):
    out = []
    for chunk in range(FULL):
        rows = slice(chunk * SPAN, (chunk + 1) * SPAN)
        out.append(dot(table[...], jnp.concatenate([h[rows] for h in halves], axis=0)))
    pad = jnp.zeros((SPAN - WPAD, halves[0].shape[1]), halves[0].dtype)
    tail = [part for h in halves for part in (h[FULL * SPAN :], pad)]
    out.append(dot(table[:WPAD, :], jnp.concatenate(tail, axis=0)))
    return jnp.concatenate(out, axis=0)


def three_parts(value):
    high = value.astype(BF)
    rest = value - high.astype(F32)
    middle = rest.astype(BF)
    low = (rest - middle.astype(F32)).astype(BF)
    return high, middle, low


def dot_exact(value, table):
    high, middle, low = three_parts(value)
    return dot(high, table) + dot(middle, table) + dot(low, table)


def stat_lanes(value, lane):
    high, middle, low = three_parts(value)
    mixed = jnp.where(
        lane < STAT + HEADS,
        high.astype(F32),
        jnp.where(lane < STAT + 2 * HEADS, middle.astype(F32), low.astype(F32)),
    )
    return jnp.where((lane >= STAT) & (lane < STAT + 3 * HEADS), mixed, 0.0)


def norm_rows(values):
    centre = values - jnp.mean(values, axis=-1, keepdims=True)
    inv_std = lax.rsqrt(jnp.mean(centre * centre, axis=-1, keepdims=True) + EPSILON)
    return (centre * inv_std, inv_std)


def place_rolled(rolled, own, ahead_d, ahead_h, ahead_dh):
    keep = SIDE - SHIFT
    rolled[:, :, SIDE:, :] = jnp.zeros((SIDE, SIDE, WPAD - SIDE, C), rolled.dtype)
    rolled[0:keep, 0:keep, 0:SIDE, :] = own[SHIFT:, SHIFT:, :, :]
    rolled[keep:, 0:keep, 0:SIDE, :] = ahead_d[...]
    rolled[0:keep, keep:, 0:SIDE, :] = ahead_h[...]
    rolled[keep:, keep:, 0:SIDE, :] = ahead_dh[...]


def pair_corner(pair):
    return WIN * lax.div(pair, 2), WIN * lax.rem(pair, 2)


def forward_pair(
    wd,
    wh,
    block,
    edges,
    wqkv,
    wturned,
    wproj,
    gather,
    scatter,
    codes,
    masks,
    rows_out,
    q_out,
    k_out,
    kt_out,
    v_out,
    mixed_out,
    mixed_t,
    stat_t,
):
    lane = lax.broadcasted_iota(jnp.int32, (1, WIDE), 1)
    in_labels = (lane >= LABEL) & (lane < LABEL + CLASSES)
    in_stats = (lane >= STAT) & (lane < STAT + 3 * HEADS)
    normed, _ = norm_rows(block.reshape(GROUP, C).astype(F32))
    pad = jnp.zeros((LROWS - ROWS, C), BF)
    both = gather_groups(gather, normed.astype(BF))
    halves = []
    for half in range(2):
        rows = jnp.concatenate([both[half].astype(BF), pad], axis=0)
        rows_out[half] = rows[:ROWS]
        q = dot(rows, wqkv[0])
        k = dot(rows, wqkv[1])
        v = dot(rows, wqkv[2])
        kt_out[half] = dot_nt(wturned[0], rows).astype(BF)[:, :ROWS]
        vt = dot_nt(wturned[1], rows).astype(BF)[:, :ROWS]
        allowed = (
            4 * jnp.where(wd == 1, edges[0], 0)
            + 2 * jnp.where(wh == 1, edges[1], 0)
            + half
            + CLASSES
        )
        here = lane == LABEL + (codes[...] & allowed)
        q_aug = jnp.where(in_labels, jnp.where(here, 1.0, 0.0), q).astype(BF)
        k_aug = jnp.where(
            in_labels, jnp.where(here, 0.0, -FAR), jnp.where(in_stats, -1.0, k)
        ).astype(BF)[:ROWS]
        v_aug = jnp.where(in_stats, -1.0, v).astype(BF)[:ROWS]
        stat_t[half] = jnp.zeros((WIDE - TILE, LROWS), F32)
        for two in range(HEADS // 2):
            q_m = jnp.concatenate(
                [q_aug * masks[h : h + 1, :] for h in (2 * two, 2 * two + 1)], axis=0
            )
            scores = dot_nt(k_aug, q_m)
            top = jnp.max(scores, axis=0, keepdims=True)
            expo = jnp.exp(scores - top)
            sums = jnp.sum(expo, axis=0, keepdims=True)
            probs = (expo * (1.0 / sums)).astype(BF)
            stats = top + jnp.log(sums)
            mixed = dot(vt[2 * HD * two : 2 * HD * (two + 1)], probs)
            for i in range(2):
                h = 2 * two + i
                lanes = slice(i * LROWS, (i + 1) * LROWS)
                mixed_t[half, h * HD : (h + 1) * HD, :] = mixed[i * HD : (i + 1) * HD, lanes]
                for part in range(3):
                    row = STAT - TILE + part * HEADS + h
                    stat_t[half, row : row + 1, :] = stats[:, lanes]
        mixed = mixed_t[half].T[:ROWS]
        mixed_out[half] = mixed
        q_out[half, :, :TILE] = q_aug[:, :TILE]
        stats = stat_lanes(stat_t[half].T, lane[:, TILE:])
        q_out[half, :, TILE:] = (q_aug[:, TILE:].astype(F32) + stats).astype(BF)
        k_out[half] = k_aug
        v_out[half] = v_aug
        halves.append(dot(mixed.astype(BF), wproj[...]).astype(BF))
    back = scatter_groups(scatter, halves).astype(BF)
    return back.reshape(WIN, WIN, WPAD, C)[:, :, :SIDE, :]


def first_block(block, own):
    block[:, :, SIDE:, :] = jnp.zeros((WIN, WIN, WPAD - SIDE, C), BF)
    block[:, :, 0:SIDE, :] = own[SHIFT : SHIFT + WIN, SHIFT : SHIFT + WIN, :, :]
    return block[...]


def forward_first(edges, own, *refs):
    *weights, out, rows, q, k, kt, v, mixed, block, mixed_t, stat_t = refs
    out[0] = forward_pair(
        0, 0, first_block(block, own), edges, *weights, rows, q, k, kt, v, mixed, mixed_t, stat_t
    )


def forward_rest(edges, own, ahead_d, ahead_h, ahead_dh, *refs):
    (
        *weights,
        out,
        slab_d,
        slab_h,
        slab_dh,
        rows,
        q,
        k,
        kt,
        v,
        mixed,
        rolled,
        mixed_t,
        stat_t,
    ) = refs
    pair = pl.program_id(0) + 1

    @pl.when(pair == 1)
    def _():
        place_rolled(rolled, own, ahead_d, ahead_h, ahead_dh)

    at_d, at_h = pair_corner(pair)
    block = rolled[pl.ds(at_d, WIN), pl.ds(at_h, WIN), :, :]
    out[0] = forward_pair(
        lax.div(pair, 2),
        lax.rem(pair, 2),
        block,
        edges,
        *weights,
        rows,
        q,
        k,
        kt,
        v,
        mixed,
        mixed_t,
        stat_t,
    )
    split = KEEP - WIN

    @pl.when(pair == 1)
    def _():
        slab_h[0:WIN] = out[0, :, split:]

    @pl.when(pair == 2)
    def _():
        slab_d[:, 0:WIN] = out[0, split:]

    @pl.when(pair == 3)
    def _():
        slab_h[WIN:] = out[0, :split, split:]
        slab_d[:, WIN:] = out[0, split:, :split]
        slab_dh[...] = out[0, split:, split:]


def backward_pair(
    block,
    rows_in,
    q_in,
    k_in,
    kt_in,
    v_in,
    mixed_in,
    wqkv,
    wproj,
    gather,
    scatter,
    masks,
    spread,
    qkv_sum,
    proj_sum,
    grad_t,
):
    lane = lax.broadcasted_iota(jnp.int32, (1, WIDE), 1)
    pad = jnp.zeros((LROWS - ROWS, C), BF)
    both = gather_groups(gather, block.reshape(GROUP, C))
    halves = []
    for half in range(2):
        grads = jnp.concatenate([both[half].astype(BF), pad], axis=0)
        mixed = mixed_in[half]
        proj_sum[...] += dot_tn(mixed.astype(BF), grads[:ROWS])
        grad_o = dot_nt(grads, wproj[...]).astype(BF)
        delta = dot_exact(mixed * grad_o[:ROWS, :C].astype(F32), spread[...])
        delta = jnp.concatenate(
            [stat_lanes(delta, lane), jnp.zeros((LROWS - ROWS, WIDE), F32)], axis=0
        )
        o_aug = (grad_o.astype(F32) + delta).astype(BF)
        q_aug = q_in[half]
        k_aug = k_in[half]
        v_aug = v_in[half]
        grad_k = jnp.zeros((ROWS, WIDE), F32)
        grad_v = jnp.zeros((ROWS, WIDE), F32)
        for two in range(HEADS // 2):
            heads = (2 * two, 2 * two + 1)
            q_m = jnp.concatenate([q_aug * masks[h : h + 1, :] for h in heads], axis=0)
            o_m = jnp.concatenate([o_aug * masks[h : h + 1, :] for h in heads], axis=0)
            probs = jnp.exp(dot_nt(k_aug, q_m))
            slopes = (probs * dot_nt(v_aug, o_m)).astype(BF)
            grad_v = grad_v + dot(probs.astype(BF), o_m)
            grad_k = grad_k + dot(slopes, q_m)
            turned = dot(kt_in[half, 2 * HD * two : 2 * HD * (two + 1), :], slopes)
            for i, h in enumerate(heads):
                grad_t[half, h * HD : (h + 1) * HD, :] = turned[
                    i * HD : (i + 1) * HD, i * LROWS : (i + 1) * LROWS
                ]
        grad_q = (grad_t[half].T[:ROWS] * HD**-0.5).astype(BF)
        grad = jnp.concatenate(
            [grad_q, grad_k[:, :C].astype(BF), grad_v[:, :C].astype(BF)], axis=1
        )
        qkv_sum[...] += dot_tn(rows_in[half], grad)
        halves.append(dot_nt(grad, wqkv[...]).astype(BF))
    back = scatter_groups(scatter, halves).astype(BF)
    return back.reshape(WIN, WIN, WPAD, C)[:, :, :SIDE, :]


def backward_first(own, *refs):
    *inputs, out, qkv_sum, proj_sum, block, grad_t = refs
    qkv_sum[...] = jnp.zeros_like(qkv_sum)
    proj_sum[...] = jnp.zeros_like(proj_sum)
    out[0] = backward_pair(first_block(block, own), *inputs, qkv_sum, proj_sum, grad_t)


def backward_rest(own, ahead_d, ahead_h, ahead_dh, *refs):
    (
        *inputs,
        qkv_in,
        proj_in,
        main,
        core,
        out,
        kept,
        given,
        rolled,
        grad_t,
        qkv_sum,
        proj_sum,
        late,
    ) = refs
    pair = pl.program_id(0) + 1

    @pl.when(pair == 1)
    def _():
        place_rolled(rolled, own, ahead_d, ahead_h, ahead_dh)
        qkv_sum[...] = qkv_in[...]
        proj_sum[...] = proj_in[...]
        late[0:MAIN, :] = main[...]
        late[MAIN + TILES * C :, :] = jnp.zeros((LATE - MAIN - TILES * C, TILE), BF)

    at_d, at_h = pair_corner(pair)
    block = rolled[pl.ds(at_d, WIN), pl.ds(at_h, WIN), :, :]
    out[0] = backward_pair(block, *inputs, qkv_sum, proj_sum, grad_t)

    @pl.when(pair == 3)
    def _():
        table = jnp.concatenate([qkv_sum[...], proj_sum[...]], axis=1).astype(BF)
        for tile in range(TILES):
            start = MAIN + tile * C
            late[start : start + C, :] = table[:, tile * TILE : (tile + 1) * TILE]
        kept[...] = late[pl.ds(core[0] * HALF, HALF), :]
        given[...] = late[pl.ds((1 - core[0]) * HALF, HALF), :]


def unpack_kernel(core, mine, other, qkv_out, proj_out, merge_out):
    first = core[0] == 0
    low = jnp.where(first, mine[...].astype(F32), other[...].astype(F32))
    high = jnp.where(first, other[...].astype(F32), mine[...].astype(F32))
    rows = 8 * C
    for tile, part in enumerate((low[:rows], low[rows:], high[:rows])):
        merge_out[:, tile * TILE : (tile + 1) * TILE] = part
    rest = high[rows:]
    table = jnp.concatenate(
        [rest[tile * C : (tile + 1) * C, :] for tile in range(TILES)], axis=1
    )
    qkv_out[...] = table[:, : 3 * C]
    proj_out[...] = table[:, 3 * C :]


def whole(shape):
    return pl.BlockSpec(shape, lambda step: (0,) * len(shape))


def per_pair(shape, first=0):
    return pl.BlockSpec(shape, lambda step: (step + first,) + (0,) * (len(shape) - 1))


KEEP = SIDE - SHIFT
GRID = (SIDE, SIDE, SIDE, C)
SLABS = ((SHIFT, KEEP, SIDE, C), (KEEP, SHIFT, SIDE, C), (SHIFT, SHIFT, SIDE, C))
SAVED = (
    ((ROWS, C), BF),
    ((LROWS, WIDE), BF),
    ((ROWS, WIDE), BF),
    ((C, ROWS), BF),
    ((ROWS, WIDE), BF),
    ((ROWS, C), F32),
)
PAIR = (1, WIN, WIN, SIDE, C)


def struct(shape, dtype):
    return jax.ShapeDtypeStruct(shape, dtype)


def call(kernel, name, count, operands, in_specs, outs, scratch, gigaflops):
    return pl.pallas_call(
        kernel,
        grid=(count,),
        in_specs=in_specs,
        out_specs=[spec for spec, _ in outs],
        out_shape=[shape for _, shape in outs],
        scratch_shapes=scratch,
        compiler_params=pltpu.CompilerParams(
            dimension_semantics=("arbitrary",), vmem_limit_bytes=VMEM_LIMIT
        ),
        cost_estimate=pl.CostEstimate(
            flops=int(gigaflops * 1e9), bytes_accessed=8 * 2**20, transcendentals=0
        ),
        name=name,
    )(*operands)


def in_hbm(array):
    return pltpu.with_memory_space_constraint(array, pltpu.HBM)


def whole_specs(arrays):
    return [whole(a.shape) for a in arrays]


def forward_call(edges, grid, slabs, weights, count):
    saved = [
        (per_pair((2,) + shape), pltpu.HBM((2 * count,) + shape, dtype))
        for shape, dtype in SAVED
    ]
    out = [(per_pair(PAIR), pltpu.HBM((count,) + PAIR[1:], BF))]
    scratch = [pltpu.VMEM((2, C, LROWS), F32), pltpu.VMEM((2, WIDE - TILE, LROWS), F32)]
    if slabs:
        out += [(whole(s), struct(s, BF)) for s in SLABS]
        scratch = [pltpu.VMEM((SIDE, SIDE, WPAD, C), BF)] + scratch
    else:
        scratch = [pltpu.VMEM((WIN, WIN, WPAD, C), BF)] + scratch
    operands = [in_hbm(grid), *slabs, *weights]
    return call(
        forward_rest if slabs else forward_first,
        "window_forward_rest" if slabs else "window_forward_first",
        count,
        [edges] + operands,
        [pl.BlockSpec(memory_space=pltpu.SMEM)] + whole_specs(operands),
        out + saved,
        scratch,
        5.0 * count,
    )


def backward_call(kernel, name, grid, slabs, saved, skip, tables, extra, count, outs, scratch, core=None):
    lead = [in_hbm(grid), *slabs]
    specs = whole_specs(lead)
    specs += [per_pair((2,) + shape, skip) for shape, _ in SAVED]
    specs += whole_specs([*tables, *extra])
    side = SIDE if slabs else WIN
    scratch = [
        pltpu.VMEM((side, side, WPAD, C), BF),
        pltpu.VMEM((2, C, LROWS), F32),
        *scratch,
    ]
    outs = [(per_pair(PAIR), pltpu.HBM((count,) + PAIR[1:], BF))] + [
        (whole(o.shape), o) for o in outs
    ]
    operands = [*lead, *[in_hbm(a) for a in (*saved, *tables)], *extra]
    if core is not None:
        operands.append(core)
        specs.append(pl.BlockSpec(memory_space=pltpu.SMEM))
    return call(kernel, name, count, operands, specs, outs, scratch, 12.0 * count)


def place_trailing(target, first, rest, behind_d, behind_h, behind_dh):
    split = KEEP - WIN
    target[SHIFT : SHIFT + WIN, SHIFT : SHIFT + WIN, 0:SIDE, :] = first[0]
    target[SHIFT : SHIFT + WIN, SHIFT + WIN :, 0:SIDE, :] = rest[0][:, :split]
    target[SHIFT + WIN :, SHIFT : SHIFT + WIN, 0:SIDE, :] = rest[1][:split]
    target[SHIFT + WIN :, SHIFT + WIN :, 0:SIDE, :] = rest[2][:split, :split]
    target[0:SHIFT, SHIFT:, 0:SIDE, :] = behind_d[...]
    target[SHIFT:, 0:SHIFT, 0:SIDE, :] = behind_h[...]
    target[0:SHIFT, 0:SHIFT, 0:SIDE, :] = behind_dh[...]


def merge_kernel(
    tokens,
    first,
    rest,
    behind_d,
    behind_h,
    behind_dh,
    cotangent,
    weight,
    gather,
    scatter,
    high_out,
    low_out,
    main_out,
    slab_d,
    slab_h,
    slab_dh,
    block,
    pieces,
):
    block[:, :, SIDE:, :] = jnp.zeros((SIDE, SIDE, WPAD - SIDE, C), BF)
    place_trailing(block, first, rest, behind_d, behind_h, behind_dh)
    block[:, :, 0:SIDE, :] = (
        tokens[...].astype(F32) + block[:, :, 0:SIDE, :].astype(F32)
    ).astype(BF)
    total = jnp.zeros((ROWS, 1), F32)
    for pair in range(4):
        a, b = pair // 2, pair % 2
        part = block[...].reshape(WIN, 2, WIN, 2, WPAD, C)[:, a, :, b]
        both = gather_groups(gather, part.reshape(GROUP, C))
        for c in range(2):
            piece = both[c]
            pieces[2 * pair + c] = piece
            total = total + jnp.sum(piece, axis=-1, keepdims=True)
    mean = total / (8 * C)
    square = jnp.zeros((ROWS, 1), F32)
    for index in range(8):
        centre = pieces[index] - mean
        square = square + jnp.sum(centre * centre, axis=-1, keepdims=True)
    inv_std = lax.rsqrt(square / (8 * C) + EPSILON)
    grad_sum = jnp.zeros((ROWS, 1), F32)
    cross_sum = jnp.zeros((ROWS, 1), F32)
    cot = cotangent[...]
    for index in range(8):
        normed = (pieces[index] - mean) * inv_std
        part = dot_tn(normed.astype(BF), cot).astype(BF)
        for tile in range(3):
            start = (tile * 8 + index) * C
            main_out[start : start + C, :] = part[:, tile * TILE : (tile + 1) * TILE]
        grad = dot_nt(cot, weight[index])
        grad_sum = grad_sum + jnp.sum(grad, axis=-1, keepdims=True)
        cross_sum = cross_sum + jnp.sum(grad * normed, axis=-1, keepdims=True)
    grad_mean = grad_sum / (8 * C)
    cross_mean = cross_sum / (8 * C)
    for a in range(2):
        highs, lows = [], []
        for b in range(2):
            high_pair, low_pair = [], []
            for c in range(2):
                index = 4 * a + 2 * b + c
                normed = (pieces[index] - mean) * inv_std
                grad = dot_nt(cot, weight[index])
                grad = inv_std * (grad - grad_mean - normed * cross_mean)
                high = grad.astype(BF)
                high_pair.append(high)
                low_pair.append((grad - high.astype(F32)).astype(BF))
            for pair, kept in ((high_pair, highs), (low_pair, lows)):
                laid = scatter_groups(scatter, pair).astype(BF)
                kept.append(laid.reshape(WIN, WIN, WPAD, C))
        for kept, out in ((highs, high_out), (lows, low_out)):
            merged = jnp.stack(kept, axis=2).reshape(WIN, SIDE, WPAD, C)
            for i in range(WIN):
                out[2 * i + a] = merged[i, :, :SIDE, :]
    slab_d[...] = high_out[:SHIFT, SHIFT:]
    slab_h[...] = high_out[SHIFT:, :SHIFT]
    slab_dh[...] = high_out[:SHIFT, :SHIFT]


def final_kernel(
    tokens, high, low, first, rest, behind_d, behind_h, behind_dh, _, out, grads
):
    place_trailing(grads, first, rest, behind_d, behind_h, behind_dh)

    @pl.loop(0, SIDE)
    def row(d):
        normed, inv_std = norm_rows(tokens[d].astype(F32))
        grad = grads[d].astype(F32)
        back = inv_std * (
            grad
            - jnp.mean(grad, axis=-1, keepdims=True)
            - normed * jnp.mean(grad * normed, axis=-1, keepdims=True)
        )
        out[d] = (high[d].astype(F32) + low[d].astype(F32) + back).astype(BF)


def merge_call(tokens, first, rest, slabs, cot_rows, weight, parity):
    operands = [in_hbm(tokens), in_hbm(first), in_hbm(rest), *slabs, cot_rows, in_hbm(weight), *parity]
    shapes = [GRID, GRID, (MAIN, TILE), *SLABS]
    kinds = [pltpu.HBM, pltpu.HBM, pltpu.HBM, struct, struct, struct]
    return call(
        merge_kernel,
        "merge_backward",
        1,
        operands,
        whole_specs(operands),
        [(whole(s), kind(s, BF)) for s, kind in zip(shapes, kinds)],
        [pltpu.VMEM((SIDE, SIDE, WPAD, C), BF), pltpu.VMEM((8, ROWS, C), F32)],
        10.0,
    )


def final_call(tokens, high, low, first, rest, slabs, after):
    operands = [in_hbm(a) for a in (tokens, high, low, first, rest)] + [*slabs]
    return call(
        final_kernel,
        "token_gradient",
        1,
        operands + [after],
        whole_specs(operands) + [pl.BlockSpec(memory_space=pl.ANY)],
        [(whole(GRID), struct(GRID, BF))],
        [pltpu.VMEM(GRID, BF)],
        7.0,
    )[0]


def moved(value, steps_d, steps_h):
    count_d, count_h = lax.axis_size("gx"), lax.axis_size("gy")
    pairs = []
    for d in range(count_d):
        for h in range(count_h):
            target = (d + steps_d) % count_d * count_h + (h + steps_h) % count_h
            pairs.append((d * count_h + h, target))
    return lax.ppermute(value, ("gx", "gy"), pairs)


def sent_back(slabs):
    d, h, dh = slabs
    return moved(d, -1, 0), moved(h, 0, -1), moved(dh, -1, -1)


def sent_on(slabs):
    d, h, dh = slabs
    return moved(d, 1, 0), moved(h, 0, 1), moved(dh, 1, 1)


def same_core():
    count_d, count_h = lax.axis_size("gx"), lax.axis_size("gy")
    return [
        [d * count_h + h for d in range(core, count_d, 2) for h in range(count_h)]
        for core in range(2)
    ]


def exchanged(blocks):
    return lax.all_to_all(
        blocks, ("gx", "gy"), 0, 0, axis_index_groups=same_core(), tiled=True
    )


def swapped(value):
    count_d, count_h = lax.axis_size("gx"), lax.axis_size("gy")
    pairs = [
        (d * count_h + h, (d ^ 1) * count_h + h) for d in range(count_d) for h in range(count_h)
    ]
    return lax.ppermute(value, ("gx", "gy"), pairs)


def block_sum(half):
    count = len(same_core()[0])
    blocks = exchanged(half.reshape(count, half.shape[0] // count, TILE))
    return jnp.sum(blocks.astype(F32), axis=0).astype(BF)


def block_spread(own):
    count = len(same_core()[0])
    spread = exchanged(jnp.broadcast_to(own[None], (count,) + own.shape))
    return spread.reshape(count * own.shape[0], TILE)


def local(tokens, qkv_weight, proj_weight, merge_weight, cotangent):
    gather = jnp.asarray(window_table(), BF)
    scatter = jnp.asarray(window_table().T, BF)
    parity = (jnp.asarray(parity_table(), BF), jnp.asarray(parity_table().T, BF))
    codes = jnp.asarray(class_codes())
    masks = jnp.asarray(head_masks(), BF)
    spread = jnp.asarray(head_spread()[:C], BF)
    edges = jnp.stack(
        [
            (lax.axis_index("gx") == lax.axis_size("gx") - 1).astype(jnp.int32),
            (lax.axis_index("gy") == lax.axis_size("gy") - 1).astype(jnp.int32),
        ]
    )
    split = qkv_weight.reshape(C, 3, C).transpose(1, 0, 2)
    scaled = jnp.concatenate([split[:1] * BF(HD**-0.5), split[1:]], axis=0)
    scaled = jnp.pad(scaled, ((0, 0), (0, 0), (0, WIDE - C)))
    turned = split[1:].transpose(0, 2, 1)
    wproj_wide = jnp.pad(proj_weight, ((0, WIDE - C), (0, 0)))
    cot_rows = jnp.pad(cotangent.reshape(TOK, 2 * C), ((0, ROWS - TOK), (0, 0)))
    weight = merge_weight.reshape(8, C, 2 * C)

    ahead = sent_back(
        (tokens[:SHIFT, SHIFT:], tokens[SHIFT:, :SHIFT], tokens[:SHIFT, :SHIFT])
    )
    weights = (scaled, turned, proj_weight, gather, scatter, codes, masks)
    first, *saved_first = forward_call(edges, tokens, (), weights, 1)
    rest, slab_d, slab_h, slab_dh, *saved_rest = forward_call(
        edges, tokens, ahead, weights, 3
    )
    high, low, main, *slabs = merge_call(
        tokens,
        first,
        rest,
        sent_on((slab_d, slab_h, slab_dh)),
        cot_rows,
        weight,
        parity,
    )
    ahead = sent_back(slabs)
    tables = (qkv_weight, wproj_wide, gather, scatter, masks, spread)
    sums = [struct((C, 3 * C), F32), struct((C, C), F32)]
    first, qkv_sum, proj_sum = backward_call(
        backward_first, "window_backward_first", high, (), saved_first, 0, tables, (), 1, sums, ()
    )
    core = lax.rem(lax.axis_index("gx"), 2).astype(jnp.int32).reshape(1)
    rest, kept, given = backward_call(
        backward_rest,
        "window_backward_rest",
        high,
        ahead,
        saved_rest,
        0,
        tables,
        (qkv_sum, proj_sum, in_hbm(main)),
        3,
        [struct((HALF, TILE), BF), struct((HALF, TILE), BF)],
        [
            pltpu.VMEM((C, 3 * C), F32),
            pltpu.VMEM((C, C), F32),
            pltpu.VMEM((LATE, TILE), BF),
        ],
        core,
    )
    half = (kept.astype(F32) + swapped(given).astype(F32)).astype(BF)
    at = KEEP - WIN
    slabs = (
        jnp.concatenate([rest[1][at:], rest[2][at:, :at]], axis=1),
        jnp.concatenate([rest[0][:, at:], rest[2][:at, at:]], axis=0),
        rest[2][at:, at:],
    )
    behind = sent_on(slabs)
    late, *behind = lax.optimization_barrier((block_sum(half), *behind))
    token_grad = final_call(tokens, high, low, first, rest, behind, late)
    late, token_grad = lax.optimization_barrier((block_spread(late), token_grad))
    shapes = [(C, 3 * C), (C, C), (8 * C, 2 * C)]
    weight_grads = call(
        unpack_kernel,
        "unpack",
        1,
        [core, late, swapped(late)],
        [pl.BlockSpec(memory_space=pltpu.SMEM)] + whole_specs([late, late]),
        [(whole(s), struct(s, F32)) for s in shapes],
        [],
        1.0,
    )
    return (token_grad, *weight_grads)


def solution(mesh):
    placed = (P("gx", "gy", None, None), P(), P(), P(), P("gx", "gy", None, None))
    return jax.shard_map(
        local,
        mesh=mesh,
        in_specs=placed,
        out_specs=(P("gx", "gy", None, None), P(), P(), P()),
        check_vma=False,
    )
```
